512 devices in a mesh: lon: 64 (over z_hi, y, core), lat: 8 (over z_lo, x).
Axes of the slice: x: 4, y: 8, z: 8 (z_hi: 4, z_lo: 2; z = z_hi * 2 + z_lo), core: 2. Of those that a mesh axis runs over, the one named last changes fastest.
Arguments:
- tokens: bfloat16 [2, 48, 768, 512], P(None, 'lat', 'lon'), may hold values from -20 to 20
- cotangent: bfloat16 [2, 48, 768, 512], P(None, 'lat', 'lon'), may hold values from -6 to 6
- w_qkv: bfloat16 [512, 1536], replicated, may hold values from -8 to 8
- w_proj: bfloat16 [512, 512], replicated, may hold values from -0.25 to 0.25
Outputs:
- d_tokens: bfloat16 [2, 48, 768, 512], P(None, 'lat', 'lon')
- d_weight: float32 [512, 1536], P('lon', 'lat')
The draws below stay inside these ranges and needn't reach their ends.
All inputs are finite; a program needn't handle non-finite values.
Results may differ from the reference program's by a relative error of at most 0.017.
The reference program's roundings to bfloat16 on the way count: a program that leaves them out, or rounds other values in their place, can miss the bound.
Values may be sent and summed in bfloat16 or wider, within the bound.
No kernel may reach another device: no remote copies, remote signals or barrier semaphores. Data moves between devices by JAX's collectives and lax.ppermute only.
A program may use at most 64 MiB of HBM per device.

```python
import math
import jax
import jax.numpy as jnp
from jax import lax

D = 512
HEADS = 16
LEV = 2
WLEV = 2
WLAT = 6
WLON = 12
NLAT = 48
NLON = 768


def draw_tokens(key, part):
    key = jax.random.fold_in(key, 11)
    first_key = jax.random.fold_in(key, 0)
    shape = (LEV, NLAT, NLON, D)
    base = jnp.clip(jax.random.normal(first_key, shape, jnp.float32), -6.0, 6.0)
    return base.astype(jnp.bfloat16)


def draw_w_qkv(key, part):
    key = jax.random.fold_in(key, 12)
    first_key = jax.random.fold_in(key, 0)
    whole = jax.random.normal(first_key, (D, 3 * D), jnp.float32) / math.sqrt(D)
    return jnp.clip(whole, -8.0, 8.0).astype(jnp.bfloat16)


def shard_levels(key, extent, cuts, low, high):
    def one(dim, blocks):
        draws = jax.random.uniform(jax.random.fold_in(jax.random.fold_in(key, 6), dim), (blocks,), jnp.float32, low / len(cuts), high / len(cuts))
        return jnp.repeat(jnp.exp(draws), extent[dim] // blocks).reshape((-1,) + (1,) * (len(extent) - dim - 1))

    gain = one(*cuts[0])
    for cut in cuts[1:]:
        gain = gain * one(*cut)
    return gain


def normal_values(key, extent, deviation, limit, shards=(), kind=jnp.bfloat16):
    array = deviation * jax.random.normal(key, extent, jnp.float32)
    if shards:
        array = array * shard_levels(key, extent, shards, -0.22, 0.18)
    return jnp.clip(array, -limit, limit).astype(kind)


def setup_inputs(seed: int = 0) -> dict:
    splits = jax.random.split(jax.random.key(seed), 5)
    tokens = draw_tokens(jax.random.fold_in(splits[4], 71), 0)
    cotangent = normal_values(splits[1], (LEV, NLAT, NLON, D), 1.0, 6.0, ((1, 8), (2, 64)))
    w_qkv = draw_w_qkv(jax.random.fold_in(splits[4], 71), 0)
    w_proj = normal_values(splits[3], (D, D), D ** -0.5, 0.25)
    return dict(tokens=tokens, cotangent=cotangent, w_qkv=w_qkv, w_proj=w_proj)


EPS = 1e-05
NEG = -1e+30

def to_windows(source):
    level_count, lat_rows, lon_cols, channels = source.shape
    shaped = source.reshape(level_count // WLEV, WLEV, lat_rows // WLAT, WLAT, lon_cols // WLON, WLON, channels)
    return shaped.transpose(0, 2, 4, 1, 3, 5, 6).reshape(-1, WLEV * WLAT * WLON, channels)

def from_windows(source, level_count, lat_rows, lon_cols):
    channels = source.shape[-1]
    shaped = source.reshape(level_count // WLEV, lat_rows // WLAT, lon_cols // WLON, WLEV, WLAT, WLON, channels)
    return shaped.transpose(0, 3, 1, 4, 2, 5, 6).reshape(level_count, lat_rows, lon_cols, channels)

def window_pass(inputs_win, grads_win, region_win, w_qkv, w_proj):
    width = w_proj.shape[0]
    head_width = width // HEADS
    window_count, length, _ = inputs_win.shape
    values32 = inputs_win.astype(jnp.float32)
    means = lax.optimization_barrier(jnp.mean(values32, axis=-1, keepdims=True))
    centred = values32 - means
    inv_std = lax.rsqrt(lax.optimization_barrier(jnp.mean(centred * centred, axis=-1, keepdims=True)) + EPS)
    unit = centred * inv_std
    flat_normed = unit.astype(jnp.bfloat16).reshape(-1, width)
    projected = jnp.dot(flat_normed, w_qkv, preferred_element_type=jnp.float32).astype(jnp.bfloat16)
    projected = projected.reshape(window_count, length, 3, HEADS, head_width)
    queries = projected[:, :, 0].astype(jnp.float32)
    key_heads = projected[:, :, 1].astype(jnp.float32)
    value_heads = projected[:, :, 2].astype(jnp.float32)
    scaling = head_width ** (-0.5)
    scores = jnp.einsum('wqhe,wkhe->whqk', queries, key_heads) * scaling
    allowed = region_win[:, :, None] == region_win[:, None, :]
    scores = jnp.where(allowed[:, None], scores, NEG)
    peak = lax.optimization_barrier(jnp.max(scores, axis=-1, keepdims=True))
    expo = jnp.exp(scores - peak)
    probs = expo / lax.optimization_barrier(jnp.sum(expo, axis=-1, keepdims=True))
    probs_low = probs.astype(jnp.bfloat16).astype(jnp.float32)
    grad_rows = grads_win.reshape(-1, width)
    d_att = jnp.dot(grad_rows, w_proj.T, preferred_element_type=jnp.float32).astype(jnp.bfloat16)
    d_att = d_att.reshape(window_count, length, HEADS, head_width).astype(jnp.float32)
    d_probs = jnp.einsum('wqhe,wkhe->whqk', d_att, value_heads)
    d_values = jnp.einsum('whqk,wqhe->wkhe', probs_low, d_att).astype(jnp.bfloat16)
    d_scores = probs * (d_probs - lax.optimization_barrier(jnp.sum(probs * d_probs, axis=-1, keepdims=True)))
    d_low = (d_scores * scaling).astype(jnp.bfloat16).astype(jnp.float32)
    d_queries = jnp.einsum('whqk,wkhe->wqhe', d_low, key_heads).astype(jnp.bfloat16)
    d_keys = jnp.einsum('whqk,wqhe->wkhe', d_low, queries).astype(jnp.bfloat16)
    d_proj = jnp.stack((d_queries, d_keys, d_values), axis=2).reshape(-1, 3 * width)
    d_normed = jnp.dot(d_proj, w_qkv.T, preferred_element_type=jnp.float32).reshape(window_count, length, width)
    d_inputs = inv_std * (d_normed - lax.optimization_barrier(jnp.mean(d_normed, axis=-1, keepdims=True)) - unit * lax.optimization_barrier(jnp.mean(d_normed * unit, axis=-1, keepdims=True)))
    return (d_inputs.astype(jnp.bfloat16), flat_normed, d_proj)

def reference(tokens, cotangent, w_qkv, w_proj):
    shifts = (-(WLEV // 2), -(WLAT // 2), -(WLON // 2))
    shifted = jnp.roll(tokens, shifts, axis=(0, 1, 2))
    moved = jnp.roll(cotangent, shifts, axis=(0, 1, 2))
    band_count = NLAT // WLAT
    band_in = jnp.moveaxis(shifted.reshape(LEV, band_count, WLAT, NLON, D), 1, 0)
    band_grad = jnp.moveaxis(moved.reshape(LEV, band_count, WLAT, NLON, D), 1, 0)
    level_region = (jnp.arange(LEV).astype(jnp.int32) >= LEV - WLEV // 2).astype(jnp.int32) * 2

    def one_band(totals, items):
        band_x, band_g, index = items
        lat_global = index * WLAT + jnp.arange(WLAT).astype(jnp.int32)
        lat_region = (lat_global >= NLAT - WLAT // 2).astype(jnp.int32)
        region = jnp.broadcast_to(level_region[:, None, None] + lat_region[None, :, None], (LEV, WLAT, NLON))
        region_win = to_windows(region[..., None])[..., 0]
        d_win, flat_normed, d_proj = window_pass(to_windows(band_x), to_windows(band_g), region_win, w_qkv, w_proj)
        totals = totals + jnp.dot(flat_normed.T, d_proj, preferred_element_type=jnp.float32)
        return (totals, from_windows(d_win, LEV, WLAT, NLON))
    totals, d_bands = lax.scan(one_band, jnp.zeros((D, 3 * D), jnp.float32), (band_in, band_grad, jnp.arange(band_count).astype(jnp.int32)))
    d_shifted = jnp.moveaxis(d_bands, 0, 1).reshape(LEV, NLAT, NLON, D)
    d_back = jnp.roll(d_shifted, (WLEV // 2, WLAT // 2, WLON // 2), axis=(0, 1, 2))
    d_tokens = (cotangent.astype(jnp.float32) + d_back.astype(jnp.float32)).astype(jnp.bfloat16)
    return (d_tokens, totals)
```

```python
import functools

import jax
import jax.numpy as jnp
from jax import lax
from jax.experimental import pallas as pl
from jax.experimental.pallas import tpu as pltpu
from jax.sharding import Mesh, PartitionSpec as P

HEADS = 16
WIDTH = 512
HEAD_WIDTH = WIDTH // HEADS
QUAD = 18
PIECE = 2 * QUAD
TOKENS = 4 * PIECE
GROUP = 8
LANES = GROUP * HEAD_WIDTH
SPREAD = GROUP * TOKENS

EPS = 1e-05
NEG = -1e30
LON = ("zh", "y", "c")
LAT = ("zl", "x")
F32 = jnp.float32
BF16 = jnp.bfloat16

NT = (((1,), (1,)), ((), ()))
TN = (((0,), (0,)), ((), ()))


def dot(a, b, dims):
    return lax.dot_general(a, b, dims, preferred_element_type=F32)


def pack_kernel(tokens_ref, grads_ref, own_ref, lat_ref, lon_ref, diag_ref, hold_ref):
    outs = ((diag_ref, lat_ref), (lon_ref, own_ref))
    for half in range(2):
        for side in range(2):
            for array, ref in enumerate((tokens_ref, grads_ref)):
                for level in range(2):
                    for row in range(3):
                        block = ref[level, 3 * half + row].astype(F32)
                        start = array * PIECE + level * QUAD + row * 6
                        hold_ref[start:start + 6, :] = block[6 * side:6 * side + 6, :]
            outs[half][side][...] = hold_ref[...].astype(BF16)


def pack(tokens, grads):
    piece = jax.ShapeDtypeStruct((2 * PIECE, WIDTH), BF16)
    return pl.pallas_call(
        pack_kernel,
        out_shape=[piece] * 4,
        scratch_shapes=[pltpu.VMEM((2 * PIECE, WIDTH), F32)],
    )(tokens, grads)


def window_kernel(
    place_ref, own_ref, lon_ref, lat_ref, diag_ref, w_qkv_ref, w_proj_ref,
    d_own_ref, d_lon_ref, d_lat_ref, d_diag_ref, keep_ref, send_ref, d_qkv_ref,
):
    pieces = [ref[...].astype(F32) for ref in (own_ref, lon_ref, lat_ref, diag_ref)]
    values = jnp.concatenate([piece[:PIECE] for piece in pieces], axis=0)
    grads = jnp.concatenate([piece[PIECE:] for piece in pieces], axis=0).astype(BF16)
    means = jnp.mean(values, axis=-1, keepdims=True)
    centred = values - means
    inv_std = lax.rsqrt(jnp.mean(centred * centred, axis=-1, keepdims=True) + EPS)
    unit = centred * inv_std
    normed = unit.astype(BF16)
    w_qkv = w_qkv_ref[...]
    qkv = jnp.dot(normed, w_qkv, preferred_element_type=F32).astype(BF16)
    d_att = dot(grads, w_proj_ref[...], NT).astype(BF16)

    last = place_ref[0]

    def region(index):
        quad = index // PIECE
        level = (index - quad * PIECE) // QUAD
        return level + jnp.where(quad >= 2, 2 * last, 0)

    key_region = region(lax.broadcasted_iota(jnp.int32, (TOKENS, 1), 0))
    query_region = region(lax.broadcasted_iota(jnp.int32, (1, SPREAD), 1) % TOKENS)
    allowed = key_region == query_region
    column_head = lax.broadcasted_iota(jnp.int32, (1, LANES), 1) // HEAD_WIDTH
    masks = [(column_head == head).astype(F32).astype(BF16) for head in range(GROUP)]
    scaling = HEAD_WIDTH ** (-0.5)

    for group in range(HEADS // GROUP):
        part = slice(group * LANES, (group + 1) * LANES)
        queries = qkv[:, part]
        keys = qkv[:, WIDTH + group * LANES:WIDTH + (group + 1) * LANES]
        vals = qkv[:, 2 * WIDTH + group * LANES:2 * WIDTH + (group + 1) * LANES]
        outer = d_att[:, part]
        queries_spread = jnp.concatenate([queries * mask for mask in masks], axis=0)
        outer_spread = jnp.concatenate([outer * mask for mask in masks], axis=0)
        scores = dot(keys, queries_spread, NT) * scaling
        scores = jnp.where(allowed, scores, NEG)
        peak = jnp.max(scores, axis=0, keepdims=True)
        expo = jnp.exp(scores - peak)
        probs = expo * (1.0 / jnp.sum(expo, axis=0, keepdims=True))
        d_probs = dot(vals, outer_spread, NT)
        d_vals = jnp.dot(probs.astype(BF16), outer_spread, preferred_element_type=F32)
        inner = jnp.sum(probs * d_probs, axis=0, keepdims=True)
        d_scores = (probs * (d_probs - inner) * scaling).astype(BF16)
        d_keys = jnp.dot(d_scores, queries_spread, preferred_element_type=F32)
        d_queries_spread = dot(d_scores, keys, TN)
        d_queries = jnp.zeros((TOKENS, LANES), F32)
        for head in range(GROUP):
            rows = d_queries_spread[head * TOKENS:(head + 1) * TOKENS]
            d_queries = jnp.where(column_head == head, rows, d_queries)
        for where, block in ((0, d_queries), (1, d_keys), (2, d_vals)):
            start = where * WIDTH + group * LANES
            d_qkv_ref[:, start:start + LANES] = block.astype(BF16)

    d_qkv = d_qkv_ref[...]
    d_normed = dot(d_qkv, w_qkv, NT)
    d_inputs = inv_std * (
        d_normed
        - jnp.mean(d_normed, axis=-1, keepdims=True)
        - unit * jnp.mean(d_normed * unit, axis=-1, keepdims=True)
    )
    for index, ref in enumerate((d_own_ref, d_lon_ref, d_lat_ref, d_diag_ref)):
        ref[...] = d_inputs[index * PIECE:(index + 1) * PIECE].astype(BF16)

    left = lax.broadcasted_iota(jnp.int32, (128, 128), 1) < 64
    core = place_ref[1]

    def write(refs):
        for pair in range(4):
            block = dot(normed, d_qkv[:, pair * 384:(pair + 1) * 384], TN)
            block = block.reshape(32, 2, 8, 384)
            for parity in range(2):
                half = block[:, parity].reshape(256, 384)
                middle = half[:, 128:256]
                turned = pltpu.roll(middle, 64, 1)
                ref = refs[parity]
                ref[2 * pair, :256, :] = half[:, :128].astype(BF16)
                ref[2 * pair, 256:, :] = jnp.where(left, middle[:128], turned[128:]).astype(BF16)
                ref[2 * pair + 1, :256, :] = half[:, 256:].astype(BF16)
                ref[2 * pair + 1, 256:, :] = jnp.where(left, turned[:128], middle[128:]).astype(BF16)

    @pl.when(core == 0)
    def _():
        write((keep_ref, send_ref))

    @pl.when(core == 1)
    def _():
        write((send_ref, keep_ref))


def window_pass(place, own, lon, lat, diag, w_qkv, w_proj):
    piece = jax.ShapeDtypeStruct((PIECE, WIDTH), BF16)
    weight = jax.ShapeDtypeStruct((8, 384, 128), BF16)
    vmem = pl.BlockSpec(memory_space=pltpu.VMEM)
    return pl.pallas_call(
        window_kernel,
        out_shape=[piece] * 4 + [weight] * 2,
        in_specs=[pl.BlockSpec(memory_space=pltpu.SMEM)] + [vmem] * 6,
        out_specs=[vmem] * 6,
        scratch_shapes=[pltpu.VMEM((TOKENS, 3 * WIDTH), BF16)],
        compiler_params=pltpu.CompilerParams(vmem_limit_bytes=40 * 1024 * 1024),
    )(place, own, lon, lat, diag, w_qkv, w_proj)


def join_kernel(grads_ref, own_ref, lon_ref, lat_ref, diag_ref, out_ref, hold_ref):
    pieces = ((diag_ref, lat_ref), (lon_ref, own_ref))
    for half in range(2):
        sides = [ref[...].astype(F32) for ref in pieces[half]]
        for level in range(2):
            for row in range(3):
                start = level * QUAD + row * 6
                for side in range(2):
                    hold_ref[6 * side:6 * side + 6, :] = sides[side][start:start + 6]
                total = grads_ref[level, 3 * half + row].astype(F32) + hold_ref[...]
                out_ref[level, 3 * half + row] = total.astype(BF16)


def join(grads, own, lon, lat, diag):
    return pl.pallas_call(
        join_kernel,
        out_shape=jax.ShapeDtypeStruct(grads.shape, BF16),
        scratch_shapes=[pltpu.VMEM((12, WIDTH), F32)],
    )(grads, own, lon, lat, diag)


def columns_kernel(parts_ref, out_ref):
    total = parts_ref[0].astype(F32)
    for index in range(1, 8):
        total = total + parts_ref[index].astype(F32)
    out_ref[:, :, :128] = total[:256].reshape(32, 8, 128).astype(BF16)
    rest = total[256:]
    out_ref[:16, :, 128:] = rest[:, :64].reshape(16, 8, 64).astype(BF16)
    out_ref[16:, :, 128:] = pltpu.roll(rest, 64, 1)[:, :64].reshape(16, 8, 64).astype(BF16)


def columns(parts):
    return pl.pallas_call(
        columns_kernel, out_shape=jax.ShapeDtypeStruct((32, 8, 192), BF16)
    )(parts)


def turn(block, axes, distance):
    count = lax.axis_size(axes)
    return lax.ppermute(block, axes, [(i, (i + distance) % count) for i in range(count)])


def turn_both(block, distance):
    lons, lats = lax.axis_size(LON), lax.axis_size(LAT)
    route = [
        (i * lats + j, (i + distance) % lons * lats + (j + distance) % lats)
        for i in range(lons)
        for j in range(lats)
    ]
    return lax.ppermute(block, LON + LAT, route)


def per_device(tokens, cotangent, w_qkv, w_proj):
    place = jnp.stack((
        (lax.axis_index(LAT) == lax.axis_size(LAT) - 1).astype(jnp.int32),
        lax.axis_index("c"),
    ))
    own, to_lat, to_lon, to_diag = pack(tokens, cotangent)
    lat = turn(to_lat, LAT, -1)
    lon = turn(to_lon, LON, -1)
    diag = turn_both(to_diag, -1)
    d_own, d_lon, d_lat, d_diag, keep, send = window_pass(
        place, own, lon, lat, diag, w_qkv, w_proj
    )
    taken = lax.ppermute(send, "c", [(0, 1), (1, 0)])
    chip = (keep.astype(F32) + taken.astype(F32)).astype(BF16)
    by_columns = lax.all_to_all(chip, LAT, 0, 0)
    by_rows = lax.all_to_all(columns(by_columns), ("zh", "y"), 0, 0)
    d_weight = jnp.sum(by_rows.astype(F32), axis=0)
    odd = lax.axis_index("x") % 2 == 1
    d_weight = jnp.where(odd, jnp.roll(d_weight, 64, axis=1), d_weight)
    d_lat = turn(d_lat, LAT, 1)
    d_lon = turn(d_lon, LON, 1)
    d_diag = turn_both(d_diag, 1)
    return (join(cotangent, d_own, d_lon, d_lat, d_diag), d_weight)


def solution(mesh):
    cut = Mesh(mesh.devices.reshape(4, 8, 2, 2, 4), LON + LAT)
    grid = P(None, LAT, LON, None)
    return jax.shard_map(
        per_device, mesh=cut, in_specs=(grid, grid, P(), P()), out_specs=(grid, P(LON, LAT)),
        check_vma=False,
    )
```

```python
import functools

import jax
import jax.numpy as jnp
from jax import lax
from jax.experimental import pallas as pl
from jax.experimental.pallas import tpu as pltpu
from jax.sharding import Mesh, PartitionSpec as P

HEADS = 16
WIDTH = 512
HEAD_WIDTH = WIDTH // HEADS
QUAD = 18
PIECE = 2 * QUAD
TOKENS = 4 * PIECE
GROUP = 8
LANES = GROUP * HEAD_WIDTH
SPREAD = GROUP * TOKENS
VMEM = 60 * 1024 * 1024
WINDOW_VMEM = 54656 * 1024
SMALL = pltpu.CompilerParams(vmem_limit_bytes=8 * 1024 * 1024)

EPS = 1e-05
NEG = -1e30
LON = ("zh", "y", "c")
LAT = ("zl", "x")
F32 = jnp.float32
BF16 = jnp.bfloat16

NT = (((1,), (1,)), ((), ()))
TN = (((0,), (0,)), ((), ()))


def dot(a, b, dims):
    return lax.dot_general(a, b, dims, preferred_element_type=F32)


def split_kernel(tokens_ref, grads_ref, own_ref, lat_ref, lon_ref, diag_ref, sems):
    copies = []
    for ref, rows, side in (
        (lat_ref, 0, 6), (lon_ref, 3, 0), (diag_ref, 0, 0), (own_ref, 3, 6)
    ):
        for array, source in enumerate((tokens_ref, grads_ref)):
            copies.append(pltpu.make_async_copy(
                source.at[rows:rows + 3, side:side + 6], ref.at[array], sems.at[len(copies)]
            ))
    for copy in copies:
        copy.start()
    for copy in copies:
        copy.wait()


def split(tokens, grads):
    anywhere = pl.BlockSpec(memory_space=pl.ANY)
    return pl.pallas_call(
        split_kernel,
        out_shape=[jax.ShapeDtypeStruct((2, 3, 6, 2, WIDTH), BF16)] * 4,
        in_specs=[anywhere] * 2,
        out_specs=[anywhere] * 4,
        scratch_shapes=[pltpu.SemaphoreType.DMA((8,))],
        compiler_params=pltpu.CompilerParams(vmem_limit_bytes=VMEM),
    )(tokens, grads)


def window_kernel(
    place_ref, own_ref, lon_ref, lat_ref, diag_ref, w_qkv_in, w_proj_in,
    d_own_ref, d_lon_ref, d_lat_ref, d_diag_ref, keep_ref, send_ref,
    d_qkv_ref, piece_ref, w_qkv_ref, w_proj_ref, weight_ref, load_sems, store_sems,
):
    loads = [
        (own_ref, piece_ref.at[0]),
        (lon_ref, piece_ref.at[1]),
        (lat_ref, piece_ref.at[2]),
        (diag_ref, piece_ref.at[3]),
        (w_qkv_in, w_qkv_ref),
        (w_proj_in, w_proj_ref),
    ]
    loads = [
        pltpu.make_async_copy(source, target, load_sems.at[index])
        for index, (source, target) in enumerate(loads)
    ]
    for load in loads:
        load.start()
    for load in loads[:4]:
        load.wait()
    pieces = [
        [piece_ref[quad, array].astype(F32).reshape(PIECE, WIDTH) for array in range(2)]
        for quad in range(4)
    ]
    values = jnp.concatenate([piece[0] for piece in pieces], axis=0)
    grads = jnp.concatenate([piece[1] for piece in pieces], axis=0).astype(BF16)
    means = jnp.mean(values, axis=-1, keepdims=True)
    centred = values - means
    inv_std = lax.rsqrt(jnp.mean(centred * centred, axis=-1, keepdims=True) + EPS)
    unit = centred * inv_std
    normed = unit.astype(BF16)
    loads[4].wait()
    w_qkv = w_qkv_ref[...]
    qkv = jnp.dot(normed, w_qkv, preferred_element_type=F32).astype(BF16)
    loads[5].wait()
    d_att = dot(grads, w_proj_ref[...], NT).astype(BF16)

    last = place_ref[0]

    def region(index):
        quad = index // PIECE
        level = index % 2
        return level + jnp.where(quad >= 2, 2 * last, 0)

    key_region = region(lax.broadcasted_iota(jnp.int32, (TOKENS, 1), 0))
    query_region = region(lax.broadcasted_iota(jnp.int32, (1, SPREAD), 1) % TOKENS)
    allowed = key_region == query_region
    column_head = lax.broadcasted_iota(jnp.int32, (1, LANES), 1) // HEAD_WIDTH
    masks = [(column_head == head).astype(F32).astype(BF16) for head in range(GROUP)]
    scaling = HEAD_WIDTH ** (-0.5)

    for group in range(HEADS // GROUP):
        part = slice(group * LANES, (group + 1) * LANES)
        queries = qkv[:, part]
        keys = qkv[:, WIDTH + group * LANES:WIDTH + (group + 1) * LANES]
        vals = qkv[:, 2 * WIDTH + group * LANES:2 * WIDTH + (group + 1) * LANES]
        outer = d_att[:, part]
        queries_spread = jnp.concatenate([queries * mask for mask in masks], axis=0)
        outer_spread = jnp.concatenate([outer * mask for mask in masks], axis=0)
        scores = dot(keys, queries_spread, NT) * scaling
        scores = jnp.where(allowed, scores, NEG)
        peak = jnp.max(scores, axis=0, keepdims=True)
        expo = jnp.exp(scores - peak)
        probs = expo * (1.0 / jnp.sum(expo, axis=0, keepdims=True))
        d_probs = dot(vals, outer_spread, NT)
        d_vals = jnp.dot(probs.astype(BF16), outer_spread, preferred_element_type=F32)
        inner = jnp.sum(probs * d_probs, axis=0, keepdims=True)
        d_scores = (probs * (d_probs - inner) * scaling).astype(BF16)
        d_keys = jnp.dot(d_scores, queries_spread, preferred_element_type=F32)
        d_queries_spread = dot(d_scores, keys, TN)
        d_queries = jnp.zeros((TOKENS, LANES), F32)
        for head in range(GROUP):
            rows = d_queries_spread[head * TOKENS:(head + 1) * TOKENS]
            d_queries = jnp.where(column_head == head, rows, d_queries)
        for where, block in ((0, d_queries), (1, d_keys), (2, d_vals)):
            start = where * WIDTH + group * LANES
            d_qkv_ref[:, start:start + LANES] = block.astype(BF16)

    d_qkv = d_qkv_ref[...]
    left = lax.broadcasted_iota(jnp.int32, (128, 128), 1) < 64
    core = place_ref[1]
    for pair in range(4):
        block = dot(normed, d_qkv[:, pair * 384:(pair + 1) * 384], TN).reshape(32, 2, 8, 384)
        for parity in range(2):
            half = block[:, parity].reshape(256, 384)
            middle = half[:, 128:256]
            turned = pltpu.roll(middle, 64, 1)
            ref = weight_ref.at[parity]
            ref[2 * pair, :256, :] = half[:, :128].astype(BF16)
            ref[2 * pair, 256:, :] = jnp.where(left, middle[:128], turned[128:]).astype(BF16)
            ref[2 * pair + 1, :256, :] = half[:, 256:].astype(BF16)
            ref[2 * pair + 1, 256:, :] = jnp.where(left, turned[:128], middle[128:]).astype(BF16)

    def stores(kept):
        return [
            pltpu.make_async_copy(weight_ref.at[parity], ref, store_sems.at[index])
            for index, (parity, ref) in enumerate(((kept, keep_ref), (1 - kept, send_ref)))
        ]

    for store in stores(core):
        store.start()
    d_normed = dot(d_qkv, w_qkv, NT)
    d_inputs = inv_std * (
        d_normed
        - jnp.mean(d_normed, axis=-1, keepdims=True)
        - unit * jnp.mean(d_normed * unit, axis=-1, keepdims=True)
    )
    for index, ref in enumerate((d_own_ref, d_lon_ref, d_lat_ref, d_diag_ref)):
        block = d_inputs[index * PIECE:(index + 1) * PIECE]
        ref[...] = block.reshape(3, 6, 2, WIDTH).astype(BF16)

    for store in stores(core):
        store.wait()


def window_pass(place, own, lon, lat, diag, w_qkv, w_proj):
    piece = jax.ShapeDtypeStruct((3, 6, 2, WIDTH), BF16)
    weight = jax.ShapeDtypeStruct((8, 384, 128), BF16)
    anywhere = pl.BlockSpec(memory_space=pl.ANY)
    return pl.pallas_call(
        window_kernel,
        out_shape=[piece] * 4 + [weight] * 2,
        in_specs=[pl.BlockSpec(memory_space=pltpu.SMEM)] + [anywhere] * 6,
        out_specs=[pl.BlockSpec(memory_space=pltpu.VMEM)] * 4 + [anywhere] * 2,
        scratch_shapes=[
            pltpu.VMEM((TOKENS, 3 * WIDTH), BF16),
            pltpu.VMEM((4, 2, 3, 6, 2, WIDTH), BF16),
            pltpu.VMEM(w_qkv.shape, BF16),
            pltpu.VMEM(w_proj.shape, BF16),
            pltpu.VMEM((2, 8, 384, 128), BF16),
            pltpu.SemaphoreType.DMA((6,)),
            pltpu.SemaphoreType.DMA((2,)),
        ],
        compiler_params=pltpu.CompilerParams(vmem_limit_bytes=WINDOW_VMEM),
    )(place, own, lon, lat, diag, w_qkv, w_proj)


def add_kernel(keep_ref, taken_ref, lon_ref, lat_ref, diag_ref, out_ref, *passed):
    out_ref[...] = (keep_ref[...].astype(F32) + taken_ref[...].astype(F32)).astype(BF16)


def add(keep, taken, *grads):
    vmem = pl.BlockSpec(memory_space=pltpu.VMEM)
    anywhere = pl.BlockSpec(memory_space=pl.ANY)
    return pl.pallas_call(
        add_kernel,
        out_shape=[jax.ShapeDtypeStruct(a.shape, a.dtype) for a in (keep,) + grads],
        in_specs=[vmem] * 2 + [anywhere] * 3,
        out_specs=[vmem] + [anywhere] * 3,
        input_output_aliases={2: 1, 3: 2, 4: 3},
        compiler_params=SMALL,
    )(keep, taken, *grads)


def join_kernel(grads_ref, own_ref, lon_ref, lat_ref, diag_ref, rows_ref, out_ref):
    for ref, rows, side in (
        (diag_ref, 0, 0), (lat_ref, 0, 6), (lon_ref, 3, 0), (own_ref, 3, 6)
    ):
        block = grads_ref[rows:rows + 3, side:side + 6].astype(F32)
        out_ref[rows:rows + 3, side:side + 6] = (block + ref[...].astype(F32)).astype(BF16)


def join(grads, own, lon, lat, diag, rows):
    vmem = pl.BlockSpec(memory_space=pltpu.VMEM)
    return pl.pallas_call(
        join_kernel,
        out_shape=jax.ShapeDtypeStruct(grads.shape, BF16),
        in_specs=[vmem] * 5 + [pl.BlockSpec(memory_space=pl.ANY)],
        out_specs=vmem,
        compiler_params=SMALL,
    )(grads, own, lon, lat, diag, rows)


def columns_kernel(parts_ref, lon_ref, lat_ref, diag_ref, out_ref):
    total = parts_ref[0].astype(F32)
    for index in range(1, 8):
        total = total + parts_ref[index].astype(F32)
    out_ref[:, :, :128] = total[:256].reshape(32, 8, 128).astype(BF16)
    rest = total[256:]
    out_ref[:16, :, 128:] = rest[:, :64].reshape(16, 8, 64).astype(BF16)
    out_ref[16:, :, 128:] = pltpu.roll(rest, 64, 1)[:, :64].reshape(16, 8, 64).astype(BF16)


def columns(parts, *grads):
    return pl.pallas_call(
        columns_kernel,
        out_shape=jax.ShapeDtypeStruct((32, 8, 192), BF16),
        in_specs=[pl.BlockSpec(memory_space=pltpu.VMEM)]
        + [pl.BlockSpec(memory_space=pl.ANY)] * 3,
        compiler_params=SMALL,
    )(parts, *grads)


def turn(block, axes, distance):
    count = lax.axis_size(axes)
    return lax.ppermute(block, axes, [(i, (i + distance) % count) for i in range(count)])


def turn_both(block, distance):
    lons, lats = lax.axis_size(LON), lax.axis_size(LAT)
    route = [
        (i * lats + j, (i + distance) % lons * lats + (j + distance) % lats)
        for i in range(lons)
        for j in range(lats)
    ]
    return lax.ppermute(block, LON + LAT, route)


def per_device(tokens, cotangent, w_qkv, w_proj):
    place = jnp.stack((
        (lax.axis_index(LAT) == lax.axis_size(LAT) - 1).astype(jnp.int32),
        lax.axis_index("c"),
    ))
    tokens = jnp.transpose(tokens, (1, 2, 0, 3))
    cotangent = jnp.transpose(cotangent, (1, 2, 0, 3))
    own, to_lat, to_lon, to_diag = split(tokens, cotangent)
    lat = turn(to_lat, LAT, -1)
    lon = turn(to_lon, LON, -1)
    diag = turn_both(to_diag, -1)
    d_own, d_lon, d_lat, d_diag, keep, send = window_pass(
        place, own, lon, lat, diag, w_qkv, w_proj
    )
    taken = lax.ppermute(send, "c", [(0, 1), (1, 0)])
    chip, d_lon, d_lat, d_diag = add(keep, taken, d_lon, d_lat, d_diag)
    by_columns = lax.all_to_all(chip, LAT, 0, 0)
    d_lat = turn(d_lat, LAT, 1)
    d_lon = turn(d_lon, LON, 1)
    d_diag = turn_both(d_diag, 1)
    rows = columns(by_columns, d_lon, d_lat, d_diag)
    by_rows = lax.all_to_all(rows, ("zh", "y"), 0, 0)
    d_tokens = join(cotangent, d_own, d_lon, d_lat, d_diag, rows)
    d_weight = jnp.sum(by_rows.astype(F32), axis=0)
    odd = lax.axis_index("x") % 2 == 1
    d_weight = jnp.where(odd, jnp.roll(d_weight, 64, axis=1), d_weight)
    return (jnp.transpose(d_tokens, (2, 0, 1, 3)), d_weight)


def solution(mesh):
    cut = Mesh(mesh.devices.reshape(4, 8, 2, 2, 4), LON + LAT)
    grid = P(None, LAT, LON, None)
    return jax.shard_map(
        per_device, mesh=cut, in_specs=(grid, grid, P(), P()), out_specs=(grid, P(LON, LAT)),
        check_vma=False,
    )
```

```python
import functools

import jax
import jax.numpy as jnp
from jax import lax
from jax.experimental import pallas as pl
from jax.experimental.pallas import tpu as pltpu
from jax.sharding import Mesh, PartitionSpec as P

HEADS = 16
WIDTH = 512
HEAD_WIDTH = WIDTH // HEADS
QUAD = 18
PIECE = 2 * QUAD
TOKENS = 4 * PIECE
GROUP = 8
LANES = GROUP * HEAD_WIDTH
SPREAD = GROUP * TOKENS
FULL = 60 * 1024 * 1024
LOAD = 51 * 1024 * 1024
WINDOW = 32 * 1024 * 1024
SMALL = pltpu.CompilerParams(vmem_limit_bytes=8 * 1024 * 1024)

EPS = 1e-05
NEG = -1e30
LON = ("zh", "y", "c")
LAT = ("zl", "x")
F32 = jnp.float32
BF16 = jnp.bfloat16

NT = (((1,), (1,)), ((), ()))
TN = (((0,), (0,)), ((), ()))


def dot(a, b, dims):
    return lax.dot_general(a, b, dims, preferred_element_type=F32)


QUARTERS = ((0, 6), (3, 0), (0, 0), (3, 6))


def split_kernel(tokens_ref, grads_ref, *refs):
    *quarter_refs, hold_ref, in_sems, out_sems = refs
    loads = [
        pltpu.make_async_copy(source, hold_ref.at[array], in_sems.at[array])
        for array, source in enumerate((tokens_ref, grads_ref))
    ]
    for load in loads:
        load.start()
    stores = []
    for array, load in enumerate(loads):
        load.wait()
        for ref, (row, side) in zip(quarter_refs, QUARTERS):
            quarter = hold_ref.at[array, row:row + 3, side:side + 6]
            store = pltpu.make_async_copy(quarter, ref.at[array], out_sems.at[len(stores)])
            store.start()
            stores.append(store)
    for store in stores:
        store.wait()


def split(tokens, grads):
    anywhere = pl.BlockSpec(memory_space=pl.ANY)
    return pl.pallas_call(
        split_kernel,
        out_shape=[jax.ShapeDtypeStruct((2, 3, 6, 2, WIDTH), BF16)] * 4,
        in_specs=[anywhere] * 2,
        out_specs=[anywhere] * 4,
        scratch_shapes=[
            pltpu.VMEM((2,) + tokens.shape, BF16),
            pltpu.SemaphoreType.DMA((2,)),
            pltpu.SemaphoreType.DMA((8,)),
        ],
        compiler_params=pltpu.CompilerParams(vmem_limit_bytes=FULL),
    )(tokens, grads)


def load_kernel(*refs):
    loads = [
        pltpu.make_async_copy(refs[index], refs[3 + index], refs[6].at[index])
        for index in range(3)
    ]
    for load in loads:
        load.start()
    for load in loads:
        load.wait()


def load(*arrays):
    return pl.pallas_call(
        load_kernel,
        out_shape=[jax.ShapeDtypeStruct(array.shape, array.dtype) for array in arrays],
        in_specs=[pl.BlockSpec(memory_space=pl.ANY)] * 3,
        out_specs=[pl.BlockSpec(memory_space=pltpu.VMEM)] * 3,
        scratch_shapes=[pltpu.SemaphoreType.DMA((3,))],
        compiler_params=pltpu.CompilerParams(vmem_limit_bytes=LOAD),
    )(*arrays)


def window_kernel(
    place_ref, own_ref, lon_ref, lat_ref, diag_ref, w_qkv_ref, w_proj_ref,
    d_own_ref, d_lon_ref, d_lat_ref, d_diag_ref, keep_ref, send_ref, d_qkv_ref,
):
    pieces = [
        [ref[array].astype(F32).reshape(PIECE, WIDTH) for array in range(2)]
        for ref in (own_ref, lon_ref, lat_ref, diag_ref)
    ]
    values = jnp.concatenate([piece[0] for piece in pieces], axis=0)
    grads = jnp.concatenate([piece[1] for piece in pieces], axis=0).astype(BF16)
    means = jnp.mean(values, axis=-1, keepdims=True)
    centred = values - means
    inv_std = lax.rsqrt(jnp.mean(centred * centred, axis=-1, keepdims=True) + EPS)
    unit = centred * inv_std
    normed = unit.astype(BF16)
    w_qkv = w_qkv_ref[...]
    qkv = jnp.dot(normed, w_qkv, preferred_element_type=F32).astype(BF16)
    d_att = dot(grads, w_proj_ref[...], NT).astype(BF16)

    last = place_ref[0]

    def region(index):
        quad = index // PIECE
        level = index % 2
        return level + jnp.where(quad >= 2, 2 * last, 0)

    key_region = region(lax.broadcasted_iota(jnp.int32, (TOKENS, 1), 0))
    query_region = region(lax.broadcasted_iota(jnp.int32, (1, SPREAD), 1) % TOKENS)
    allowed = key_region == query_region
    column_head = lax.broadcasted_iota(jnp.int32, (1, LANES), 1) // HEAD_WIDTH
    masks = [(column_head == head).astype(F32).astype(BF16) for head in range(GROUP)]
    scaling = HEAD_WIDTH ** (-0.5)

    for group in range(HEADS // GROUP):
        part = slice(group * LANES, (group + 1) * LANES)
        queries = qkv[:, part]
        keys = qkv[:, WIDTH + group * LANES:WIDTH + (group + 1) * LANES]
        vals = qkv[:, 2 * WIDTH + group * LANES:2 * WIDTH + (group + 1) * LANES]
        outer = d_att[:, part]
        queries_spread = jnp.concatenate([queries * mask for mask in masks], axis=0)
        outer_spread = jnp.concatenate([outer * mask for mask in masks], axis=0)
        scores = dot(keys, queries_spread, NT) * scaling
        scores = jnp.where(allowed, scores, NEG)
        peak = jnp.max(scores, axis=0, keepdims=True)
        expo = jnp.exp(scores - peak)
        probs = expo * (1.0 / jnp.sum(expo, axis=0, keepdims=True))
        d_probs = dot(vals, outer_spread, NT)
        d_vals = jnp.dot(probs.astype(BF16), outer_spread, preferred_element_type=F32)
        inner = jnp.sum(probs * d_probs, axis=0, keepdims=True)
        d_scores = (probs * (d_probs - inner) * scaling).astype(BF16)
        d_keys = jnp.dot(d_scores, queries_spread, preferred_element_type=F32)
        d_queries_spread = dot(d_scores, keys, TN)
        d_queries = jnp.zeros((TOKENS, LANES), F32)
        for head in range(GROUP):
            rows = d_queries_spread[head * TOKENS:(head + 1) * TOKENS]
            d_queries = jnp.where(column_head == head, rows, d_queries)
        for where, block in ((0, d_queries), (1, d_keys), (2, d_vals)):
            start = where * WIDTH + group * LANES
            d_qkv_ref[:, start:start + LANES] = block.astype(BF16)

    d_qkv = d_qkv_ref[...]
    left = lax.broadcasted_iota(jnp.int32, (128, 128), 1) < 64
    core = place_ref[1]

    def write(refs):
        for pair in range(4):
            block = dot(normed, d_qkv[:, pair * 384:(pair + 1) * 384], TN).reshape(32, 2, 8, 384)
            for parity, ref in enumerate(refs):
                half = block[:, parity].reshape(256, 384)
                middle = half[:, 128:256]
                turned = pltpu.roll(middle, 64, 1)
                folded = (
                    jnp.where(left, middle[:128], turned[128:]),
                    jnp.where(left, turned[:128], middle[128:]),
                )
                for side in range(2):
                    ref[2 * pair + side, :256, :] = half[:, 256 * side:256 * side + 128].astype(BF16)
                    ref[2 * pair + side, 256:, :] = folded[side].astype(BF16)

    @pl.when(core == 0)
    def _():
        write((keep_ref, send_ref))

    @pl.when(core == 1)
    def _():
        write((send_ref, keep_ref))

    d_normed = dot(d_qkv, w_qkv, NT)
    d_inputs = inv_std * (
        d_normed
        - jnp.mean(d_normed, axis=-1, keepdims=True)
        - unit * jnp.mean(d_normed * unit, axis=-1, keepdims=True)
    )
    for index, ref in enumerate((d_own_ref, d_lon_ref, d_lat_ref, d_diag_ref)):
        block = d_inputs[index * PIECE:(index + 1) * PIECE]
        ref[...] = block.reshape(3, 6, 2, WIDTH).astype(BF16)


def window_pass(place, own, lon, lat, diag, w_qkv, w_proj):
    piece = jax.ShapeDtypeStruct((3, 6, 2, WIDTH), BF16)
    weight = jax.ShapeDtypeStruct((8, 384, 128), BF16)
    vmem = pl.BlockSpec(memory_space=pltpu.VMEM)
    return pl.pallas_call(
        window_kernel,
        out_shape=[piece] * 4 + [weight] * 2,
        in_specs=[pl.BlockSpec(memory_space=pltpu.SMEM)] + [vmem] * 6,
        out_specs=[vmem] * 6,
        scratch_shapes=[pltpu.VMEM((TOKENS, 3 * WIDTH), BF16)],
        compiler_params=pltpu.CompilerParams(vmem_limit_bytes=WINDOW),
    )(place, own, lon, lat, diag, w_qkv, w_proj)


def add_kernel(keep_ref, taken_ref, lon_ref, lat_ref, diag_ref, out_ref, *passed):
    out_ref[...] = (keep_ref[...].astype(F32) + taken_ref[...].astype(F32)).astype(BF16)


def add(keep, taken, *grads):
    vmem = pl.BlockSpec(memory_space=pltpu.VMEM)
    anywhere = pl.BlockSpec(memory_space=pl.ANY)
    return pl.pallas_call(
        add_kernel,
        out_shape=[jax.ShapeDtypeStruct(a.shape, a.dtype) for a in (keep,) + grads],
        in_specs=[vmem] * 2 + [anywhere] * 3,
        out_specs=[vmem] + [anywhere] * 3,
        input_output_aliases={2: 1, 3: 2, 4: 3},
        compiler_params=SMALL,
    )(keep, taken, *grads)


def join_kernel(grads_ref, own_ref, lon_ref, lat_ref, diag_ref, rows_ref, out_ref):
    for ref, rows, side in (
        (diag_ref, 0, 0), (lat_ref, 0, 6), (lon_ref, 3, 0), (own_ref, 3, 6)
    ):
        block = grads_ref[rows:rows + 3, side:side + 6].astype(F32)
        out_ref[rows:rows + 3, side:side + 6] = (block + ref[...].astype(F32)).astype(BF16)


def join(grads, own, lon, lat, diag, rows):
    vmem = pl.BlockSpec(memory_space=pltpu.VMEM)
    return pl.pallas_call(
        join_kernel,
        out_shape=jax.ShapeDtypeStruct(grads.shape, BF16),
        in_specs=[vmem] * 5 + [pl.BlockSpec(memory_space=pl.ANY)],
        out_specs=vmem,
        compiler_params=SMALL,
    )(grads, own, lon, lat, diag, rows)


def columns_kernel(parts_ref, diag_in, lon_ref, lat_ref, out_ref, diag_out):
    total = parts_ref[0].astype(F32)
    for index in range(1, 8):
        total = total + parts_ref[index].astype(F32)
    out_ref[:, :, :128] = total[:256].reshape(32, 8, 128).astype(BF16)
    rest = total[256:]
    out_ref[:16, :, 128:] = rest[:, :64].reshape(16, 8, 64).astype(BF16)
    out_ref[16:, :, 128:] = pltpu.roll(rest, 64, 1)[:, :64].reshape(16, 8, 64).astype(BF16)


def columns(parts, diag, lon, lat):
    vmem = pl.BlockSpec(memory_space=pltpu.VMEM)
    anywhere = pl.BlockSpec(memory_space=pl.ANY)
    return pl.pallas_call(
        columns_kernel,
        out_shape=[
            jax.ShapeDtypeStruct((32, 8, 192), BF16), jax.ShapeDtypeStruct(diag.shape, BF16)
        ],
        in_specs=[vmem] + [anywhere] * 3,
        out_specs=[vmem, anywhere],
        input_output_aliases={1: 1},
        compiler_params=SMALL,
    )(parts, diag, lon, lat)


def turn(block, axes, distance):
    count = lax.axis_size(axes)
    return lax.ppermute(block, axes, [(i, (i + distance) % count) for i in range(count)])


def turn_both(block, distance):
    lons, lats = lax.axis_size(LON), lax.axis_size(LAT)
    route = [
        (i * lats + j, (i + distance) % lons * lats + (j + distance) % lats)
        for i in range(lons)
        for j in range(lats)
    ]
    return lax.ppermute(block, LON + LAT, route)


def per_device(tokens, cotangent, w_qkv, w_proj):
    place = jnp.stack((
        (lax.axis_index(LAT) == lax.axis_size(LAT) - 1).astype(jnp.int32),
        lax.axis_index("c"),
    ))
    tokens = jnp.transpose(tokens, (1, 2, 0, 3))
    cotangent = jnp.transpose(cotangent, (1, 2, 0, 3))
    to_lat, to_lon, to_diag, own = split(tokens, cotangent)
    lat = turn(to_lat, LAT, -1)
    lon = turn(to_lon, LON, -1)
    diag = turn_both(to_diag, -1)
    own, w_qkv, w_proj = load(own, w_qkv, w_proj)
    d_own, d_lon, d_lat, d_diag, keep, send = window_pass(
        place, own, lon, lat, diag, w_qkv, w_proj
    )
    taken = lax.ppermute(send, "c", [(0, 1), (1, 0)])
    chip, d_lon, d_lat, d_diag = add(keep, taken, d_lon, d_lat, d_diag)
    by_columns = lax.all_to_all(chip, LAT, 0, 0)
    d_lat = turn(d_lat, LAT, 1)
    d_lon = turn(d_lon, LON, 1)
    rows, d_diag = columns(by_columns, d_diag, d_lon, d_lat)
    by_rows = lax.all_to_all(rows, ("zh", "y"), 0, 0)
    d_diag = turn_both(d_diag, 1)
    d_tokens = join(cotangent, d_own, d_lon, d_lat, d_diag, rows)
    d_weight = jnp.sum(by_rows.astype(F32), axis=0)
    odd = lax.axis_index("x") % 2 == 1
    d_weight = jnp.where(odd, jnp.roll(d_weight, 64, axis=1), d_weight)
    return (jnp.transpose(d_tokens, (2, 0, 1, 3)), d_weight)


def solution(mesh):
    cut = Mesh(mesh.devices.reshape(4, 8, 2, 2, 4), LON + LAT)
    grid = P(None, LAT, LON, None)
    return jax.shard_map(
        per_device, mesh=cut, in_specs=(grid, grid, P(), P()), out_specs=(grid, P(LON, LAT)),
        check_vma=False,
    )
```

```python
import functools

import jax
import jax.numpy as jnp
from jax import lax
from jax.experimental import pallas as pl
from jax.experimental.pallas import tpu as pltpu
from jax.sharding import Mesh, PartitionSpec as P

HEADS = 16
WIDTH = 512
HEAD_WIDTH = WIDTH // HEADS
QUAD = 18
PIECE = 2 * QUAD
TOKENS = 4 * PIECE
GROUP = 8
LANES = GROUP * HEAD_WIDTH
SPREAD = GROUP * TOKENS
FULL = 54880 * 1024
LOAD = 51 * 1024 * 1024
WINDOW = 32 * 1024 * 1024
SMALL = pltpu.CompilerParams(vmem_limit_bytes=8 * 1024 * 1024)

EPS = 1e-05
NEG = -1e30
LON = ("zh", "y", "c")
LAT = ("zl", "x")
F32 = jnp.float32
BF16 = jnp.bfloat16

NT = (((1,), (1,)), ((), ()))
TN = (((0,), (0,)), ((), ()))


def dot(a, b, dims):
    return lax.dot_general(a, b, dims, preferred_element_type=F32)


QUARTERS = ((3, 6), (0, 6), (3, 0), (0, 0))


def split_kernel(tokens_ref, grads_ref, *refs):
    *quarter_refs, sems = refs
    copies = []
    for ref, (row, side) in zip(quarter_refs, QUARTERS):
        for array, source in enumerate((tokens_ref, grads_ref)):
            quarter = source.at[row:row + 3, side:side + 6]
            copies.append(pltpu.make_async_copy(quarter, ref.at[array], sems.at[len(copies)]))
    for copy in copies:
        copy.start()
    for copy in copies:
        copy.wait()


def split(tokens, grads):
    return pl.pallas_call(
        split_kernel,
        out_shape=[jax.ShapeDtypeStruct((2, 3, 6, 2, WIDTH), BF16)] * 4,
        in_specs=[pl.BlockSpec(memory_space=pl.ANY)] * 2,
        out_specs=[pl.BlockSpec(memory_space=pltpu.VMEM)] * 4,
        scratch_shapes=[pltpu.SemaphoreType.DMA((8,))],
        compiler_params=pltpu.CompilerParams(vmem_limit_bytes=FULL),
    )(tokens, grads)


def load_kernel(*refs):
    loads = [
        pltpu.make_async_copy(refs[index], refs[2 + index], refs[4].at[index])
        for index in range(2)
    ]
    for load in loads:
        load.start()
    for load in loads:
        load.wait()


def load(*arrays):
    return pl.pallas_call(
        load_kernel,
        out_shape=[jax.ShapeDtypeStruct(array.shape, array.dtype) for array in arrays],
        in_specs=[pl.BlockSpec(memory_space=pl.ANY)] * 2,
        out_specs=[pl.BlockSpec(memory_space=pltpu.VMEM)] * 2,
        scratch_shapes=[pltpu.SemaphoreType.DMA((2,))],
        compiler_params=pltpu.CompilerParams(vmem_limit_bytes=LOAD),
    )(*arrays)


def window_kernel(
    place_ref, diag_ref, lat_ref, lon_ref, own_ref, w_qkv_ref, w_proj_ref,
    keep_ref, send_ref, d_qkv_ref, unit_ref, inv_std_ref,
):
    pieces = [
        [ref[array].astype(F32).reshape(PIECE, WIDTH) for array in range(2)]
        for ref in (own_ref, lon_ref, lat_ref, diag_ref)
    ]
    values = jnp.concatenate([piece[0] for piece in pieces], axis=0)
    grads = jnp.concatenate([piece[1] for piece in pieces], axis=0).astype(BF16)
    means = jnp.mean(values, axis=-1, keepdims=True)
    centred = values - means
    inv_std = lax.rsqrt(jnp.mean(centred * centred, axis=-1, keepdims=True) + EPS)
    unit = centred * inv_std
    unit_ref[...] = unit
    inv_std_ref[...] = jnp.broadcast_to(inv_std, inv_std_ref.shape)
    normed = unit.astype(BF16)
    qkv = jnp.dot(normed, w_qkv_ref[...], preferred_element_type=F32).astype(BF16)
    d_att = dot(grads, w_proj_ref[...], NT).astype(BF16)

    last = place_ref[0]

    def region(index):
        quad = index // PIECE
        level = index % 2
        return level + jnp.where(quad >= 2, 2 * last, 0)

    key_region = region(lax.broadcasted_iota(jnp.int32, (TOKENS, 1), 0))
    query_region = region(lax.broadcasted_iota(jnp.int32, (1, SPREAD), 1) % TOKENS)
    allowed = key_region == query_region
    column_head = lax.broadcasted_iota(jnp.int32, (1, LANES), 1) // HEAD_WIDTH
    masks = [(column_head == head).astype(F32).astype(BF16) for head in range(GROUP)]
    scaling = HEAD_WIDTH ** (-0.5)

    for group in range(HEADS // GROUP):
        part = slice(group * LANES, (group + 1) * LANES)
        queries = qkv[:, part]
        keys = qkv[:, WIDTH + group * LANES:WIDTH + (group + 1) * LANES]
        vals = qkv[:, 2 * WIDTH + group * LANES:2 * WIDTH + (group + 1) * LANES]
        outer = d_att[:, part]
        queries_spread = jnp.concatenate([queries * mask for mask in masks], axis=0)
        outer_spread = jnp.concatenate([outer * mask for mask in masks], axis=0)
        scores = dot(keys, queries_spread, NT) * scaling
        scores = jnp.where(allowed, scores, NEG)
        peak = jnp.max(scores, axis=0, keepdims=True)
        expo = jnp.exp(scores - peak)
        probs = expo * (1.0 / jnp.sum(expo, axis=0, keepdims=True))
        d_probs = dot(vals, outer_spread, NT)
        d_vals = jnp.dot(probs.astype(BF16), outer_spread, preferred_element_type=F32)
        inner = jnp.sum(probs * d_probs, axis=0, keepdims=True)
        d_scores = (probs * (d_probs - inner) * scaling).astype(BF16)
        d_keys = jnp.dot(d_scores, queries_spread, preferred_element_type=F32)
        d_queries_spread = dot(d_scores, keys, TN)
        d_queries = jnp.zeros((TOKENS, LANES), F32)
        for head in range(GROUP):
            rows = d_queries_spread[head * TOKENS:(head + 1) * TOKENS]
            d_queries = jnp.where(column_head == head, rows, d_queries)
        for where, block in ((0, d_queries), (1, d_keys), (2, d_vals)):
            start = where * WIDTH + group * LANES
            d_qkv_ref[:, start:start + LANES] = block.astype(BF16)

    d_qkv = d_qkv_ref[...]
    left = lax.broadcasted_iota(jnp.int32, (128, 128), 1) < 64
    core = place_ref[1]

    def write(refs):
        for pair in range(4):
            block = dot(normed, d_qkv[:, pair * 384:(pair + 1) * 384], TN).reshape(32, 2, 8, 384)
            for parity, ref in enumerate(refs):
                half = block[:, parity].reshape(256, 384)
                middle = half[:, 128:256]
                turned = pltpu.roll(middle, 64, 1)
                folded = (
                    jnp.where(left, middle[:128], turned[128:]),
                    jnp.where(left, turned[:128], middle[128:]),
                )
                for side in range(2):
                    ref[2 * pair + side, :256, :] = half[:, 256 * side:256 * side + 128].astype(BF16)
                    ref[2 * pair + side, 256:, :] = folded[side].astype(BF16)

    @pl.when(core == 0)
    def _():
        write((keep_ref, send_ref))

    @pl.when(core == 1)
    def _():
        write((send_ref, keep_ref))


def window_pass(place, diag, lat, lon, own, w_qkv, w_proj):
    weight = jax.ShapeDtypeStruct((8, 384, 128), BF16)
    vmem = pl.BlockSpec(memory_space=pltpu.VMEM)
    return pl.pallas_call(
        window_kernel,
        out_shape=[weight] * 2 + [
            jax.ShapeDtypeStruct((TOKENS, 3 * WIDTH), BF16),
            jax.ShapeDtypeStruct((TOKENS, WIDTH), F32),
            jax.ShapeDtypeStruct((TOKENS, 128), F32),
        ],
        in_specs=[pl.BlockSpec(memory_space=pltpu.SMEM)] + [vmem] * 6,
        out_specs=[vmem] * 5,
        compiler_params=pltpu.CompilerParams(vmem_limit_bytes=WINDOW),
    )(place, diag, lat, lon, own, w_qkv, w_proj)


def inputs_kernel(
    d_qkv_ref, unit_ref, inv_std_ref, w_qkv_ref, d_own_ref, d_side_ref, d_lat_ref
):
    unit = unit_ref[...]
    d_normed = dot(d_qkv_ref[...], w_qkv_ref[...], NT)
    d_inputs = inv_std_ref[:, :1] * (
        d_normed
        - jnp.mean(d_normed, axis=-1, keepdims=True)
        - unit * jnp.mean(d_normed * unit, axis=-1, keepdims=True)
    )
    d_refs = (d_own_ref, d_side_ref.at[0], d_lat_ref, d_side_ref.at[1])
    for index, ref in enumerate(d_refs):
        block = d_inputs[index * PIECE:(index + 1) * PIECE]
        ref[...] = block.reshape(3, 6, 2, WIDTH).astype(BF16)


def inputs_pass(d_qkv, unit, inv_std, w_qkv):
    piece = jax.ShapeDtypeStruct((3, 6, 2, WIDTH), BF16)
    side = jax.ShapeDtypeStruct((2, 3, 6, 2, WIDTH), BF16)
    return pl.pallas_call(
        inputs_kernel, out_shape=[piece, side, piece], compiler_params=SMALL
    )(d_qkv, unit, inv_std, w_qkv)


def add_kernel(keep_ref, taken_ref, side_in, out_ref, side_out):
    out_ref[...] = (keep_ref[...].astype(F32) + taken_ref[...].astype(F32)).astype(BF16)


def add(keep, taken, side):
    vmem = pl.BlockSpec(memory_space=pltpu.VMEM)
    anywhere = pl.BlockSpec(memory_space=pl.ANY)
    return pl.pallas_call(
        add_kernel,
        out_shape=[jax.ShapeDtypeStruct(a.shape, a.dtype) for a in (keep, side)],
        in_specs=[vmem] * 2 + [anywhere],
        out_specs=[vmem, anywhere],
        input_output_aliases={2: 1},
        compiler_params=SMALL,
    )(keep, taken, side)


def join_kernel(grads_ref, own_ref, side_ref, ahead_ref, out_ref):
    for ref, row, side in (
        (ahead_ref.at[1], 3, 6), (side_ref.at[0], 0, 6), (ahead_ref.at[0], 3, 0), (own_ref, 0, 0)
    ):
        block = grads_ref[row:row + 3, side:side + 6].astype(F32)
        out_ref[row:row + 3, side:side + 6] = (block + ref[...].astype(F32)).astype(BF16)


def join(grads, own, side, ahead):
    return pl.pallas_call(
        join_kernel, out_shape=jax.ShapeDtypeStruct(grads.shape, BF16), compiler_params=SMALL
    )(grads, own, side, ahead)


def columns_kernel(parts_ref, lat_in, out_ref, lat_out):
    total = parts_ref[0].astype(F32)
    for index in range(1, 8):
        total = total + parts_ref[index].astype(F32)
    out_ref[:, :, :128] = total[:256].reshape(32, 8, 128).astype(BF16)
    rest = total[256:]
    out_ref[:16, :, 128:] = rest[:, :64].reshape(16, 8, 64).astype(BF16)
    out_ref[16:, :, 128:] = pltpu.roll(rest, 64, 1)[:, :64].reshape(16, 8, 64).astype(BF16)


def columns(parts, lat):
    vmem = pl.BlockSpec(memory_space=pltpu.VMEM)
    anywhere = pl.BlockSpec(memory_space=pl.ANY)
    return pl.pallas_call(
        columns_kernel,
        out_shape=[
            jax.ShapeDtypeStruct((32, 8, 192), BF16), jax.ShapeDtypeStruct(lat.shape, BF16)
        ],
        in_specs=[vmem, anywhere],
        out_specs=[vmem, anywhere],
        input_output_aliases={1: 1},
        compiler_params=SMALL,
    )(parts, lat)


def turn(block, axes, distance):
    count = lax.axis_size(axes)
    return lax.ppermute(block, axes, [(i, (i + distance) % count) for i in range(count)])


def turn_both(block, distance):
    lons, lats = lax.axis_size(LON), lax.axis_size(LAT)
    route = [
        (i * lats + j, (i + distance) % lons * lats + (j + distance) % lats)
        for i in range(lons)
        for j in range(lats)
    ]
    return lax.ppermute(block, LON + LAT, route)


def per_device(tokens, cotangent, w_qkv, w_proj):
    place = jnp.stack((
        (lax.axis_index(LAT) == 0).astype(jnp.int32),
        lax.axis_index("c"),
    ))
    tokens = jnp.transpose(tokens, (1, 2, 0, 3))
    cotangent = jnp.transpose(cotangent, (1, 2, 0, 3))
    to_diag, to_lon, to_lat, own = split(tokens, cotangent)
    diag = turn_both(to_diag, 1)
    lon = turn(to_lon, LON, 1)
    lat = turn(to_lat, LAT, 1)
    w_qkv, w_proj = load(w_qkv, w_proj)
    keep, send, d_qkv, unit, inv_std = window_pass(place, diag, lat, lon, own, w_qkv, w_proj)
    taken = lax.ppermute(send, "c", [(0, 1), (1, 0)])
    d_own, d_side, d_lat = inputs_pass(d_qkv, unit, inv_std, w_qkv)
    chip, d_side = add(keep, taken, d_side)
    by_columns = lax.all_to_all(chip, LAT, 0, 0)
    d_side = turn(d_side, LON, -1)
    rows, d_lat = columns(by_columns, d_lat)
    by_rows = lax.all_to_all(rows, ("zh", "y"), 0, 0)
    d_ahead = turn(jnp.stack((d_lat, d_side[1])), LAT, -1)
    d_tokens = join(cotangent, d_own, d_side, d_ahead)
    d_weight = jnp.sum(by_rows.astype(F32), axis=0)
    odd = lax.axis_index("x") % 2 == 1
    d_weight = jnp.where(odd, jnp.roll(d_weight, 64, axis=1), d_weight)
    return (jnp.transpose(d_tokens, (2, 0, 1, 3)), d_weight)


def solution(mesh):
    cut = Mesh(mesh.devices.reshape(4, 8, 2, 2, 4), LON + LAT)
    grid = P(None, LAT, LON, None)
    return jax.shard_map(
        per_device, mesh=cut, in_specs=(grid, grid, P(), P()), out_specs=(grid, P(LON, LAT)),
        check_vma=False,
    )
```

```python
import functools

import jax
import jax.numpy as jnp
from jax import lax
from jax.experimental import pallas as pl
from jax.experimental.pallas import tpu as pltpu
from jax.sharding import Mesh, PartitionSpec as P

HEADS = 16
WIDTH = 512
HEAD_WIDTH = WIDTH // HEADS
QUAD = 18
PIECE = 2 * QUAD
TOKENS = 4 * PIECE
GROUP = 8
LANES = GROUP * HEAD_WIDTH
SPREAD = GROUP * TOKENS
FULL = 54880 * 1024
LOAD = 51 * 1024 * 1024
WINDOW = 32 * 1024 * 1024
SMALL = pltpu.CompilerParams(vmem_limit_bytes=8 * 1024 * 1024)

EPS = 1e-05
NEG = -1e30
LON = ("zh", "y", "c")
LAT = ("zl", "x")
LON_ORDER = [31 - i for i in range(32)]
F32 = jnp.float32
BF16 = jnp.bfloat16

NT = (((1,), (1,)), ((), ()))
TN = (((0,), (0,)), ((), ()))


def dot(a, b, dims):
    return lax.dot_general(a, b, dims, preferred_element_type=F32)


QUARTERS = ((3, 6), (0, 6), (3, 0), (0, 0))


def split_kernel(tokens_ref, grads_ref, *refs):
    *quarter_refs, sems = refs
    copies = []
    for ref, (row, side) in zip(quarter_refs, QUARTERS):
        for array, source in enumerate((tokens_ref, grads_ref)):
            quarter = source.at[row:row + 3, side:side + 6]
            copies.append(pltpu.make_async_copy(quarter, ref.at[array], sems.at[len(copies)]))
    for copy in copies:
        copy.start()
    for copy in copies:
        copy.wait()


def split(tokens, grads):
    return pl.pallas_call(
        split_kernel,
        out_shape=[jax.ShapeDtypeStruct((2, 3, 6, 2, WIDTH), BF16)] * 4,
        in_specs=[pl.BlockSpec(memory_space=pl.ANY)] * 2,
        out_specs=[pl.BlockSpec(memory_space=pltpu.VMEM)] * 4,
        scratch_shapes=[pltpu.SemaphoreType.DMA((8,))],
        compiler_params=pltpu.CompilerParams(vmem_limit_bytes=FULL),
    )(tokens, grads)


def load_kernel(*refs):
    loads = [
        pltpu.make_async_copy(refs[index], refs[2 + index], refs[4].at[index])
        for index in range(2)
    ]
    for load in loads:
        load.start()
    for load in loads:
        load.wait()


def load(*arrays):
    return pl.pallas_call(
        load_kernel,
        out_shape=[jax.ShapeDtypeStruct(array.shape, array.dtype) for array in arrays],
        in_specs=[pl.BlockSpec(memory_space=pl.ANY)] * 2,
        out_specs=[pl.BlockSpec(memory_space=pltpu.VMEM)] * 2,
        scratch_shapes=[pltpu.SemaphoreType.DMA((2,))],
        compiler_params=pltpu.CompilerParams(vmem_limit_bytes=LOAD),
    )(*arrays)


def window_kernel(
    place_ref, diag_ref, lat_ref, lon_ref, own_ref, w_qkv_ref, w_proj_ref,
    send_ref, d_qkv_ref, unit_ref, turned_ref, inv_std_ref,
):
    pieces = [
        [ref[array].astype(F32).reshape(PIECE, WIDTH) for array in range(2)]
        for ref in (own_ref, lon_ref, lat_ref, diag_ref)
    ]
    values = jnp.concatenate([piece[0] for piece in pieces], axis=0)
    grads = jnp.concatenate([piece[1] for piece in pieces], axis=0).astype(BF16)
    means = jnp.mean(values, axis=-1, keepdims=True)
    centred = values - means
    inv_std = lax.rsqrt(jnp.mean(centred * centred, axis=-1, keepdims=True) + EPS)
    unit = centred * inv_std
    unit_ref[...] = unit
    turned_ref[...] = unit.T.reshape(turned_ref.shape)
    inv_std_ref[...] = jnp.broadcast_to(inv_std, inv_std_ref.shape)
    normed = unit.astype(BF16)
    qkv = jnp.dot(normed, w_qkv_ref[...], preferred_element_type=F32).astype(BF16)
    d_att = dot(grads, w_proj_ref[...], NT).astype(BF16)

    last = place_ref[0]

    def region(index):
        quad = index // PIECE
        level = index % 2
        return level + jnp.where(quad >= 2, 2 * last, 0)

    key_region = region(lax.broadcasted_iota(jnp.int32, (TOKENS, 1), 0))
    query_region = region(lax.broadcasted_iota(jnp.int32, (1, SPREAD), 1) % TOKENS)
    allowed = key_region == query_region
    column_head = lax.broadcasted_iota(jnp.int32, (1, LANES), 1) // HEAD_WIDTH
    masks = [(column_head == head).astype(F32).astype(BF16) for head in range(GROUP)]
    scaling = HEAD_WIDTH ** (-0.5)

    for group in range(HEADS // GROUP):
        part = slice(group * LANES, (group + 1) * LANES)
        queries = qkv[:, part]
        keys = qkv[:, WIDTH + group * LANES:WIDTH + (group + 1) * LANES]
        vals = qkv[:, 2 * WIDTH + group * LANES:2 * WIDTH + (group + 1) * LANES]
        outer = d_att[:, part]
        queries_spread = jnp.concatenate([queries * mask for mask in masks], axis=0)
        outer_spread = jnp.concatenate([outer * mask for mask in masks], axis=0)
        scores = dot(keys, queries_spread, NT) * scaling
        scores = jnp.where(allowed, scores, NEG)
        peak = jnp.max(scores, axis=0, keepdims=True)
        expo = jnp.exp(scores - peak)
        probs = expo * (1.0 / jnp.sum(expo, axis=0, keepdims=True))
        d_probs = dot(vals, outer_spread, NT)
        d_vals = jnp.dot(probs.astype(BF16), outer_spread, preferred_element_type=F32)
        inner = jnp.sum(probs * d_probs, axis=0, keepdims=True)
        d_scores = (probs * (d_probs - inner) * scaling).astype(BF16)
        d_keys = jnp.dot(d_scores, queries_spread, preferred_element_type=F32)
        d_queries_spread = dot(d_scores, keys, TN)
        d_queries = jnp.zeros((TOKENS, LANES), F32)
        for head in range(GROUP):
            rows = d_queries_spread[head * TOKENS:(head + 1) * TOKENS]
            d_queries = jnp.where(column_head == head, rows, d_queries)
        for where, block in ((0, d_queries), (1, d_keys), (2, d_vals)):
            start = where * WIDTH + group * LANES
            d_qkv_ref[:, start:start + LANES] = block.astype(BF16)

    weight_rows(turned_ref, 1 - place_ref[1], d_qkv_ref, send_ref)


def weight_rows(turned_ref, core, d_qkv_ref, out_ref):
    turned = turned_ref[:, pl.ds(core, 1)].reshape(WIDTH // 2, TOKENS).astype(BF16)
    left = lax.broadcasted_iota(jnp.int32, (128, 128), 1) < 64
    for pair in range(4):
        columns = d_qkv_ref[:, pair * 384:(pair + 1) * 384]
        block = jnp.dot(turned, columns, preferred_element_type=F32)
        middle = block[:, 128:256]
        swapped = pltpu.roll(middle, 64, 1)
        folded = (
            jnp.where(left, middle[:128], swapped[128:]),
            jnp.where(left, swapped[:128], middle[128:]),
        )
        for side in range(2):
            whole = block[:, 256 * side:256 * side + 128]
            place = 2 * pair + side
            out_ref[place, :256, :] = whole.astype(BF16)
            out_ref[place, 256:, :] = folded[side].astype(BF16)


def window_pass(place, diag, lat, lon, own, w_qkv, w_proj):
    weight = jax.ShapeDtypeStruct((8, 384, 128), BF16)
    vmem = pl.BlockSpec(memory_space=pltpu.VMEM)
    return pl.pallas_call(
        window_kernel,
        out_shape=[
            weight,
            jax.ShapeDtypeStruct((TOKENS, 3 * WIDTH), BF16),
            jax.ShapeDtypeStruct((TOKENS, WIDTH), F32),
            jax.ShapeDtypeStruct((WIDTH // 16, 2, 8, TOKENS), F32),
            jax.ShapeDtypeStruct((TOKENS, 128), F32),
        ],
        in_specs=[pl.BlockSpec(memory_space=pltpu.SMEM)] + [vmem] * 6,
        out_specs=[vmem] * 5,
        compiler_params=pltpu.CompilerParams(vmem_limit_bytes=WINDOW),
    )(place, diag, lat, lon, own, w_qkv, w_proj)


def inputs_kernel(
    place_ref, d_qkv_ref, unit_ref, turned_ref, inv_std_ref, w_qkv_ref,
    keep_ref, d_own_ref, d_side_ref, d_lat_ref,
):
    weight_rows(turned_ref, place_ref[1], d_qkv_ref, keep_ref)
    unit = unit_ref[...]
    d_normed = dot(d_qkv_ref[...], w_qkv_ref[...], NT)
    d_inputs = inv_std_ref[:, :1] * (
        d_normed
        - jnp.mean(d_normed, axis=-1, keepdims=True)
        - unit * jnp.mean(d_normed * unit, axis=-1, keepdims=True)
    )
    d_refs = (d_own_ref, d_side_ref.at[0], d_lat_ref, d_side_ref.at[1])
    for index, ref in enumerate(d_refs):
        block = d_inputs[index * PIECE:(index + 1) * PIECE]
        ref[...] = block.reshape(3, 6, 2, WIDTH).astype(BF16)


def inputs_pass(place, d_qkv, unit, turned, inv_std, w_qkv):
    weight = jax.ShapeDtypeStruct((8, 384, 128), BF16)
    piece = jax.ShapeDtypeStruct((3, 6, 2, WIDTH), BF16)
    side = jax.ShapeDtypeStruct((2, 3, 6, 2, WIDTH), BF16)
    return pl.pallas_call(
        inputs_kernel,
        out_shape=[weight, piece, side, piece],
        in_specs=[pl.BlockSpec(memory_space=pltpu.SMEM)]
        + [pl.BlockSpec(memory_space=pltpu.VMEM)] * 5,
        compiler_params=SMALL,
    )(place, d_qkv, unit, turned, inv_std, w_qkv)


def add_kernel(keep_ref, taken_ref, side_in, out_ref, side_out, hold_ref, sems):
    stores = []
    for index in range(8):
        total = keep_ref[index].astype(F32) + taken_ref[index].astype(F32)
        hold_ref[index] = total.astype(BF16)
        store = pltpu.make_async_copy(hold_ref.at[index], out_ref.at[index], sems.at[index])
        store.start()
        stores.append(store)
    for store in stores:
        store.wait()


def add(keep, taken, side):
    vmem = pl.BlockSpec(memory_space=pltpu.VMEM)
    anywhere = pl.BlockSpec(memory_space=pl.ANY)
    return pl.pallas_call(
        add_kernel,
        out_shape=[jax.ShapeDtypeStruct(a.shape, a.dtype) for a in (keep, side)],
        in_specs=[vmem] * 2 + [anywhere],
        out_specs=[anywhere] * 2,
        input_output_aliases={2: 1},
        scratch_shapes=[pltpu.VMEM(keep.shape, BF16), pltpu.SemaphoreType.DMA((8,))],
        compiler_params=SMALL,
    )(keep, taken, side)


def join_kernel(grads_ref, own_ref, side_ref, ahead_ref, out_ref):
    for ref, row, side in (
        (ahead_ref.at[1], 3, 6), (side_ref.at[0], 0, 6), (ahead_ref.at[0], 3, 0), (own_ref, 0, 0)
    ):
        block = grads_ref[row:row + 3, side:side + 6].astype(F32)
        out_ref[row:row + 3, side:side + 6] = (block + ref[...].astype(F32)).astype(BF16)


def join(grads, own, side, ahead):
    return pl.pallas_call(
        join_kernel, out_shape=jax.ShapeDtypeStruct(grads.shape, BF16), compiler_params=SMALL
    )(grads, own, side, ahead)


def columns_kernel(parts_ref, lat_in, out_ref, lat_out):
    total = parts_ref[0].astype(F32)
    for index in range(1, 8):
        total = total + parts_ref[index].astype(F32)
    rests = (total[256:], pltpu.roll(total[256:], 64, 1))
    for tile in range(32):
        row, fold = 8 * tile, 256 + 8 * (tile % 16)
        place = LON_ORDER.index(tile)
        out_ref[place, :, :128] = total[row:row + 8].astype(BF16)
        out_ref[place, :, 128:] = rests[tile // 16][fold - 256:fold - 248, :64].astype(BF16)


def columns(parts, lat):
    vmem = pl.BlockSpec(memory_space=pltpu.VMEM)
    anywhere = pl.BlockSpec(memory_space=pl.ANY)
    return pl.pallas_call(
        columns_kernel,
        out_shape=[
            jax.ShapeDtypeStruct((32, 8, 192), BF16), jax.ShapeDtypeStruct(lat.shape, BF16)
        ],
        in_specs=[vmem, anywhere],
        out_specs=[vmem, anywhere],
        input_output_aliases={1: 1},
        compiler_params=SMALL,
    )(parts, lat)


def turn(block, axes, distance):
    count = lax.axis_size(axes)
    return lax.ppermute(block, axes, [(i, (i + distance) % count) for i in range(count)])


def turn_both(block, distance):
    lons, lats = lax.axis_size(LON), lax.axis_size(LAT)
    route = [
        (i * lats + j, (i + distance) % lons * lats + (j + distance) % lats)
        for i in range(lons)
        for j in range(lats)
    ]
    return lax.ppermute(block, LON + LAT, route)


def per_device(tokens, cotangent, w_qkv, w_proj):
    place = jnp.stack((
        (lax.axis_index(LAT) == 0).astype(jnp.int32),
        lax.axis_index("c"),
    ))
    tokens = jnp.transpose(tokens, (1, 2, 0, 3))
    cotangent = jnp.transpose(cotangent, (1, 2, 0, 3))
    to_diag, to_lon, to_lat, own = split(tokens, cotangent)
    diag = turn_both(to_diag, 1)
    lon = turn(to_lon, LON, 1)
    lat = turn(to_lat, LAT, 1)
    w_qkv, w_proj = load(w_qkv, w_proj)
    send, *saved = window_pass(place, diag, lat, lon, own, w_qkv, w_proj)
    taken = lax.ppermute(send, "c", [(0, 1), (1, 0)])
    keep, d_own, d_side, d_lat = inputs_pass(place, *saved, w_qkv)
    chip, d_side = add(keep, taken, d_side)
    by_columns = lax.all_to_all(chip, LAT, 0, 0)
    d_side = turn(d_side, LON, -1)
    rows, d_lat = columns(by_columns, d_lat)
    groups = [[2 * tile + core for tile in LON_ORDER] for core in range(2)]
    by_rows = lax.all_to_all(rows, LON, 0, 0, axis_index_groups=groups)
    d_ahead = turn(jnp.stack((d_lat, d_side[1])), LAT, -1)
    d_tokens = join(cotangent, d_own, d_side, d_ahead)
    d_weight = jnp.sum(by_rows.astype(F32), axis=0)
    odd = lax.axis_index("x") % 2 == 1
    d_weight = jnp.where(odd, jnp.roll(d_weight, 64, axis=1), d_weight)
    return (jnp.transpose(d_tokens, (2, 0, 1, 3)), d_weight)


def solution(mesh):
    cut = Mesh(mesh.devices.reshape(4, 8, 2, 2, 4), LON + LAT)
    grid = P(None, LAT, LON, None)
    return jax.shard_map(
        per_device, mesh=cut, in_specs=(grid, grid, P(), P()), out_specs=(grid, P(LON, LAT)),
        check_vma=False,
    )
```

```python
import functools

import jax
import jax.numpy as jnp
from jax import lax
from jax.experimental import pallas as pl
from jax.experimental.pallas import tpu as pltpu
from jax.sharding import Mesh, PartitionSpec as P

HEADS = 16
WIDTH = 512
HEAD_WIDTH = WIDTH // HEADS
QUAD = 18
PIECE = 2 * QUAD
TOKENS = 4 * PIECE
GROUP = 8
LANES = GROUP * HEAD_WIDTH
SPREAD = GROUP * TOKENS
FULL = 54880 * 1024
LOAD = 51 * 1024 * 1024
WINDOW = 32 * 1024 * 1024
SMALL = pltpu.CompilerParams(vmem_limit_bytes=8 * 1024 * 1024)

EPS = 1e-05
NEG = -1e30
LON = ("zh", "y", "c")
LAT = ("zl", "x")
LON_ORDER = [31 - i for i in range(32)]
F32 = jnp.float32
BF16 = jnp.bfloat16

NT = (((1,), (1,)), ((), ()))
TN = (((0,), (0,)), ((), ()))


def dot(a, b, dims):
    return lax.dot_general(a, b, dims, preferred_element_type=F32)


QUARTERS = ((3, 6), (0, 6), (3, 0), (0, 0))


def split_kernel(tokens_ref, grads_ref, *refs):
    *quarter_refs, sems = refs
    copies = []
    for ref, (row, side) in zip(quarter_refs, QUARTERS):
        for array, source in enumerate((tokens_ref, grads_ref)):
            quarter = source.at[row:row + 3, side:side + 6]
            copies.append(pltpu.make_async_copy(quarter, ref.at[array], sems.at[len(copies)]))
    for copy in copies:
        copy.start()
    for copy in copies:
        copy.wait()


def split(tokens, grads):
    return pl.pallas_call(
        split_kernel,
        out_shape=[jax.ShapeDtypeStruct((2, 3, 6, 2, WIDTH), BF16)] * 4,
        in_specs=[pl.BlockSpec(memory_space=pl.ANY)] * 2,
        out_specs=[pl.BlockSpec(memory_space=pltpu.VMEM)] * 4,
        scratch_shapes=[pltpu.SemaphoreType.DMA((8,))],
        compiler_params=pltpu.CompilerParams(vmem_limit_bytes=FULL),
    )(tokens, grads)


def load_kernel(*refs):
    loads = [
        pltpu.make_async_copy(refs[index], refs[2 + index], refs[4].at[index])
        for index in range(2)
    ]
    for load in loads:
        load.start()
    for load in loads:
        load.wait()


def load(*arrays):
    return pl.pallas_call(
        load_kernel,
        out_shape=[jax.ShapeDtypeStruct(array.shape, array.dtype) for array in arrays],
        in_specs=[pl.BlockSpec(memory_space=pl.ANY)] * 2,
        out_specs=[pl.BlockSpec(memory_space=pltpu.VMEM)] * 2,
        scratch_shapes=[pltpu.SemaphoreType.DMA((2,))],
        compiler_params=pltpu.CompilerParams(vmem_limit_bytes=LOAD),
    )(*arrays)


def window_kernel(
    diag_ref, lat_ref, lon_ref, own_ref, w_qkv_ref, w_proj_ref,
    send_ref, d_qkv_ref, unit_ref, turned_ref, inv_std_ref,
):
    pieces = [
        [ref[array].astype(F32).reshape(PIECE, WIDTH) for array in range(2)]
        for ref in (own_ref, lon_ref, lat_ref, diag_ref)
    ]
    values = jnp.concatenate([piece[0] for piece in pieces], axis=0)
    grads = jnp.concatenate([piece[1] for piece in pieces], axis=0).astype(BF16)
    means = jnp.mean(values, axis=-1, keepdims=True)
    centred = values - means
    inv_std = lax.rsqrt(jnp.mean(centred * centred, axis=-1, keepdims=True) + EPS)
    unit = centred * inv_std
    unit_ref[...] = unit
    turned_ref[...] = unit.T.reshape(turned_ref.shape)
    inv_std_ref[...] = jnp.broadcast_to(inv_std, inv_std_ref.shape)
    normed = unit.astype(BF16)
    qkv = jnp.dot(normed, w_qkv_ref[...], preferred_element_type=F32).astype(BF16)
    d_att = dot(grads, w_proj_ref[...], NT).astype(BF16)

    last = (lax.axis_index(LAT) == 0).astype(jnp.int32)

    def region(index):
        quad = index // PIECE
        level = index % 2
        return level + jnp.where(quad >= 2, 2 * last, 0)

    key_region = region(lax.broadcasted_iota(jnp.int32, (TOKENS, 1), 0))
    query_region = region(lax.broadcasted_iota(jnp.int32, (1, SPREAD), 1) % TOKENS)
    allowed = key_region == query_region
    column_head = lax.broadcasted_iota(jnp.int32, (1, LANES), 1) // HEAD_WIDTH
    masks = [(column_head == head).astype(F32).astype(BF16) for head in range(GROUP)]
    scaling = HEAD_WIDTH ** (-0.5)

    for group in range(HEADS // GROUP):
        part = slice(group * LANES, (group + 1) * LANES)
        queries = qkv[:, part]
        keys = qkv[:, WIDTH + group * LANES:WIDTH + (group + 1) * LANES]
        vals = qkv[:, 2 * WIDTH + group * LANES:2 * WIDTH + (group + 1) * LANES]
        outer = d_att[:, part]
        queries_spread = jnp.concatenate([queries * mask for mask in masks], axis=0)
        outer_spread = jnp.concatenate([outer * mask for mask in masks], axis=0)
        scores = dot(keys, queries_spread, NT) * scaling
        scores = jnp.where(allowed, scores, NEG)
        peak = jnp.max(scores, axis=0, keepdims=True)
        expo = jnp.exp(scores - peak)
        probs = expo * (1.0 / jnp.sum(expo, axis=0, keepdims=True))
        d_probs = dot(vals, outer_spread, NT)
        d_vals = jnp.dot(probs.astype(BF16), outer_spread, preferred_element_type=F32)
        inner = jnp.sum(probs * d_probs, axis=0, keepdims=True)
        d_scores = (probs * (d_probs - inner) * scaling).astype(BF16)
        d_keys = jnp.dot(d_scores, queries_spread, preferred_element_type=F32)
        d_queries_spread = dot(d_scores, keys, TN)
        d_queries = jnp.zeros((TOKENS, LANES), F32)
        for head in range(GROUP):
            rows = d_queries_spread[head * TOKENS:(head + 1) * TOKENS]
            d_queries = jnp.where(column_head == head, rows, d_queries)
        for where, block in ((0, d_queries), (1, d_keys), (2, d_vals)):
            start = where * WIDTH + group * LANES
            d_qkv_ref[:, start:start + LANES] = block.astype(BF16)

    weight_rows(turned_ref, 1 - lax.axis_index("c"), d_qkv_ref, send_ref)


def weight_rows(turned_ref, core, d_qkv_ref, out_ref):
    turned = turned_ref[:, pl.ds(core, 1)].reshape(WIDTH // 2, TOKENS).astype(BF16)
    left = lax.broadcasted_iota(jnp.int32, (128, 128), 1) < 64
    for pair in range(4):
        columns = d_qkv_ref[:, pair * 384:(pair + 1) * 384]
        block = jnp.dot(turned, columns, preferred_element_type=F32)
        middle = block[:, 128:256]
        swapped = pltpu.roll(middle, 64, 1)
        folded = (
            jnp.where(left, middle[:128], swapped[128:]),
            jnp.where(left, swapped[:128], middle[128:]),
        )
        for side in range(2):
            whole = block[:, 256 * side:256 * side + 128]
            place = 2 * pair + side
            out_ref[place, :256, :] = whole.astype(BF16)
            out_ref[place, 256:, :] = folded[side].astype(BF16)


def window_pass(diag, lat, lon, own, w_qkv, w_proj):
    weight = jax.ShapeDtypeStruct((8, 384, 128), BF16)
    vmem = pl.BlockSpec(memory_space=pltpu.VMEM)
    return pl.pallas_call(
        window_kernel,
        out_shape=[
            weight,
            jax.ShapeDtypeStruct((TOKENS, 3 * WIDTH), BF16),
            jax.ShapeDtypeStruct((TOKENS, WIDTH), F32),
            jax.ShapeDtypeStruct((WIDTH // 16, 2, 8, TOKENS), F32),
            jax.ShapeDtypeStruct((TOKENS, 128), F32),
        ],
        in_specs=[vmem] * 6,
        out_specs=[vmem] * 5,
        compiler_params=pltpu.CompilerParams(vmem_limit_bytes=WINDOW),
    )(diag, lat, lon, own, w_qkv, w_proj)


def inputs_kernel(
    d_qkv_ref, unit_ref, turned_ref, inv_std_ref, w_qkv_ref,
    keep_ref, d_own_ref, d_side_ref, d_lat_ref,
):
    weight_rows(turned_ref, lax.axis_index("c"), d_qkv_ref, keep_ref)
    unit = unit_ref[...]
    d_normed = dot(d_qkv_ref[...], w_qkv_ref[...], NT)
    d_inputs = inv_std_ref[:, :1] * (
        d_normed
        - jnp.mean(d_normed, axis=-1, keepdims=True)
        - unit * jnp.mean(d_normed * unit, axis=-1, keepdims=True)
    )
    d_refs = (d_own_ref, d_side_ref.at[0], d_lat_ref, d_side_ref.at[1])
    for index, ref in enumerate(d_refs):
        block = d_inputs[index * PIECE:(index + 1) * PIECE]
        ref[...] = block.reshape(3, 6, 2, WIDTH).astype(BF16)


def inputs_pass(d_qkv, unit, turned, inv_std, w_qkv):
    weight = jax.ShapeDtypeStruct((8, 384, 128), BF16)
    piece = jax.ShapeDtypeStruct((3, 6, 2, WIDTH), BF16)
    side = jax.ShapeDtypeStruct((2, 3, 6, 2, WIDTH), BF16)
    return pl.pallas_call(
        inputs_kernel,
        out_shape=[weight, piece, side, piece],
        compiler_params=SMALL,
    )(d_qkv, unit, turned, inv_std, w_qkv)


def add_kernel(keep_ref, taken_ref, side_in, out_ref, side_out, hold_ref, sems):
    stores = []
    for index in range(8):
        total = keep_ref[index].astype(F32) + taken_ref[index].astype(F32)
        hold_ref[index] = total.astype(BF16)
        store = pltpu.make_async_copy(hold_ref.at[index], out_ref.at[index], sems.at[index])
        store.start()
        stores.append(store)
    for store in stores:
        store.wait()


def add(keep, taken, side):
    vmem = pl.BlockSpec(memory_space=pltpu.VMEM)
    anywhere = pl.BlockSpec(memory_space=pl.ANY)
    return pl.pallas_call(
        add_kernel,
        out_shape=[jax.ShapeDtypeStruct(a.shape, a.dtype) for a in (keep, side)],
        in_specs=[vmem] * 2 + [anywhere],
        out_specs=[anywhere] * 2,
        input_output_aliases={2: 1},
        scratch_shapes=[pltpu.VMEM(keep.shape, BF16), pltpu.SemaphoreType.DMA((8,))],
        compiler_params=SMALL,
    )(keep, taken, side)


def finish_kernel(
    grads_ref, own_ref, side_ref, ahead_ref, rows_ref, d_tokens_ref, d_weight_ref
):
    for ref, row, side in (
        (ahead_ref.at[1], 3, 6), (side_ref.at[0], 0, 6), (ahead_ref.at[0], 3, 0), (own_ref, 0, 0)
    ):
        block = grads_ref[row:row + 3, side:side + 6].astype(F32)
        d_tokens_ref[row:row + 3, side:side + 6] = (block + ref[...].astype(F32)).astype(BF16)
    total = jnp.sum(rows_ref[...].astype(F32), axis=0)

    odd = lax.axis_index("x") % 2

    @pl.when(odd == 0)
    def _():
        d_weight_ref[...] = total

    @pl.when(odd == 1)
    def _():
        d_weight_ref[:, :64] = total[:, 128:]
        d_weight_ref[:, 64:] = total[:, :128]


def finish(grads, own, side, ahead, rows):
    return pl.pallas_call(
        finish_kernel,
        out_shape=[
            jax.ShapeDtypeStruct(grads.shape, BF16), jax.ShapeDtypeStruct(rows.shape[1:], F32)
        ],
        compiler_params=SMALL,
    )(grads, own, side, ahead, rows)


def columns_kernel(parts_ref, lat_in, out_ref, lat_out):
    total = parts_ref[0].astype(F32)
    for index in range(1, 8):
        total = total + parts_ref[index].astype(F32)
    rests = (total[256:], pltpu.roll(total[256:], 64, 1))
    for tile in range(32):
        row, fold = 8 * tile, 256 + 8 * (tile % 16)
        place = LON_ORDER.index(tile)
        out_ref[place, :, :128] = total[row:row + 8].astype(BF16)
        out_ref[place, :, 128:] = rests[tile // 16][fold - 256:fold - 248, :64].astype(BF16)


def columns(parts, lat):
    vmem = pl.BlockSpec(memory_space=pltpu.VMEM)
    anywhere = pl.BlockSpec(memory_space=pl.ANY)
    return pl.pallas_call(
        columns_kernel,
        out_shape=[
            jax.ShapeDtypeStruct((32, 8, 192), BF16), jax.ShapeDtypeStruct(lat.shape, BF16)
        ],
        in_specs=[vmem, anywhere],
        out_specs=[vmem, anywhere],
        input_output_aliases={1: 1},
        compiler_params=SMALL,
    )(parts, lat)


def turn(block, axes, distance):
    count = lax.axis_size(axes)
    return lax.ppermute(block, axes, [(i, (i + distance) % count) for i in range(count)])


def turn_both(block, distance):
    lons, lats = lax.axis_size(LON), lax.axis_size(LAT)
    route = [
        (i * lats + j, (i + distance) % lons * lats + (j + distance) % lats)
        for i in range(lons)
        for j in range(lats)
    ]
    return lax.ppermute(block, LON + LAT, route)


def per_device(tokens, cotangent, w_qkv, w_proj):
    tokens = jnp.transpose(tokens, (1, 2, 0, 3))
    cotangent = jnp.transpose(cotangent, (1, 2, 0, 3))
    to_diag, to_lon, to_lat, own = split(tokens, cotangent)
    diag = turn_both(to_diag, 1)
    lon = turn(to_lon, LON, 1)
    lat = turn(to_lat, LAT, 1)
    w_qkv, w_proj = load(w_qkv, w_proj)
    send, *saved = window_pass(diag, lat, lon, own, w_qkv, w_proj)
    taken = lax.ppermute(send, "c", [(0, 1), (1, 0)])
    keep, d_own, d_side, d_lat = inputs_pass(*saved, w_qkv)
    chip, d_side = add(keep, taken, d_side)
    by_columns = lax.all_to_all(chip, LAT, 0, 0)
    d_side = turn(d_side, LON, -1)
    rows, d_lat = columns(by_columns, d_lat)
    groups = [[2 * tile + core for tile in LON_ORDER] for core in range(2)]
    by_rows = lax.all_to_all(rows, LON, 0, 0, axis_index_groups=groups)
    d_ahead = turn(jnp.stack((d_lat, d_side[1])), LAT, -1)
    d_tokens, d_weight = finish(cotangent, d_own, d_side, d_ahead, by_rows)
    return (jnp.transpose(d_tokens, (2, 0, 1, 3)), d_weight)


def solution(mesh):
    cut = Mesh(mesh.devices.reshape(4, 8, 2, 2, 4), LON + LAT)
    grid = P(None, LAT, LON, None)
    return jax.shard_map(
        per_device, mesh=cut, in_specs=(grid, grid, P(), P()), out_specs=(grid, P(LON, LAT)),
        check_vma=False,
    )
```

```python
import functools

import jax
import jax.numpy as jnp
from jax import lax
from jax.experimental import pallas as pl
from jax.experimental.pallas import tpu as pltpu
from jax.sharding import Mesh, PartitionSpec as P

HEADS = 16
WIDTH = 512
HEAD_WIDTH = WIDTH // HEADS
QUAD = 18
PIECE = 2 * QUAD
TOKENS = 4 * PIECE
GROUP = 8
LANES = GROUP * HEAD_WIDTH
SPREAD = GROUP * TOKENS
FULL = 54880 * 1024
LOAD = 51 * 1024 * 1024
WINDOW = 32 * 1024 * 1024
SMALL = pltpu.CompilerParams(vmem_limit_bytes=8 * 1024 * 1024)

EPS = 1e-05
NEG = -1e30
LON = ("zh", "y", "c")
LAT = ("zl", "x")
LON_ORDER = [31 - i for i in range(32)]
F32 = jnp.float32
BF16 = jnp.bfloat16

NT = (((1,), (1,)), ((), ()))
TN = (((0,), (0,)), ((), ()))


def dot(a, b, dims):
    return lax.dot_general(a, b, dims, preferred_element_type=F32)


QUARTERS = ((3, 6), (0, 6), (3, 0), (0, 0))


def split_kernel(tokens_ref, grads_ref, *refs):
    *quarter_refs, sems = refs
    copies = []
    for ref, (row, side) in zip(quarter_refs, QUARTERS):
        for array, source in enumerate((tokens_ref, grads_ref)):
            quarter = source.at[row:row + 3, side:side + 6]
            copies.append(pltpu.make_async_copy(quarter, ref.at[array], sems.at[len(copies)]))
    for copy in copies:
        copy.start()
    for copy in copies:
        copy.wait()


def split(tokens, grads):
    return pl.pallas_call(
        split_kernel,
        out_shape=[jax.ShapeDtypeStruct((2, 3, 6, 2, WIDTH), BF16)] * 4,
        in_specs=[pl.BlockSpec(memory_space=pl.ANY)] * 2,
        out_specs=[pl.BlockSpec(memory_space=pltpu.VMEM)] * 4,
        scratch_shapes=[pltpu.SemaphoreType.DMA((8,))],
        compiler_params=pltpu.CompilerParams(vmem_limit_bytes=FULL),
    )(tokens, grads)


def load_kernel(*refs):
    loads = [
        pltpu.make_async_copy(refs[index], refs[2 + index], refs[4].at[index])
        for index in range(2)
    ]
    for load in loads:
        load.start()
    for load in loads:
        load.wait()


def load(*arrays):
    return pl.pallas_call(
        load_kernel,
        out_shape=[jax.ShapeDtypeStruct(array.shape, array.dtype) for array in arrays],
        in_specs=[pl.BlockSpec(memory_space=pl.ANY)] * 2,
        out_specs=[pl.BlockSpec(memory_space=pltpu.VMEM)] * 2,
        scratch_shapes=[pltpu.SemaphoreType.DMA((2,))],
        compiler_params=pltpu.CompilerParams(vmem_limit_bytes=LOAD),
    )(*arrays)


def window_kernel(
    diag_ref, lat_ref, lon_ref, own_ref, w_qkv_ref, w_proj_ref,
    factors_ref, unit_ref, inv_std_ref,
):
    pieces = [
        [ref[array].astype(F32).reshape(PIECE, WIDTH) for array in range(2)]
        for ref in (own_ref, lon_ref, lat_ref, diag_ref)
    ]
    values = jnp.concatenate([piece[0] for piece in pieces], axis=0)
    grads = jnp.concatenate([piece[1] for piece in pieces], axis=0).astype(BF16)
    means = jnp.mean(values, axis=-1, keepdims=True)
    centred = values - means
    inv_std = lax.rsqrt(jnp.mean(centred * centred, axis=-1, keepdims=True) + EPS)
    unit = centred * inv_std
    unit_ref[...] = unit
    inv_std_ref[...] = jnp.broadcast_to(inv_std, inv_std_ref.shape)
    normed = unit.astype(BF16)
    factors_ref[:, 3 * WIDTH:] = normed
    qkv = jnp.dot(normed, w_qkv_ref[...], preferred_element_type=F32).astype(BF16)
    d_att = dot(grads, w_proj_ref[...], NT).astype(BF16)

    last = (lax.axis_index(LAT) == 0).astype(jnp.int32)

    def region(index):
        quad = index // PIECE
        level = index % 2
        return level + jnp.where(quad >= 2, 2 * last, 0)

    key_region = region(lax.broadcasted_iota(jnp.int32, (TOKENS, 1), 0))
    query_region = region(lax.broadcasted_iota(jnp.int32, (1, SPREAD), 1) % TOKENS)
    allowed = key_region == query_region
    column_head = lax.broadcasted_iota(jnp.int32, (1, LANES), 1) // HEAD_WIDTH
    masks = [(column_head == head).astype(F32).astype(BF16) for head in range(GROUP)]
    scaling = HEAD_WIDTH ** (-0.5)

    for group in range(HEADS // GROUP):
        part = slice(group * LANES, (group + 1) * LANES)
        queries = qkv[:, part]
        keys = qkv[:, WIDTH + group * LANES:WIDTH + (group + 1) * LANES]
        vals = qkv[:, 2 * WIDTH + group * LANES:2 * WIDTH + (group + 1) * LANES]
        outer = d_att[:, part]
        queries_spread = jnp.concatenate([queries * mask for mask in masks], axis=0)
        outer_spread = jnp.concatenate([outer * mask for mask in masks], axis=0)
        scores = dot(keys, queries_spread, NT) * scaling
        scores = jnp.where(allowed, scores, NEG)
        peak = jnp.max(scores, axis=0, keepdims=True)
        expo = jnp.exp(scores - peak)
        probs = expo * (1.0 / jnp.sum(expo, axis=0, keepdims=True))
        d_probs = dot(vals, outer_spread, NT)
        d_vals = jnp.dot(probs.astype(BF16), outer_spread, preferred_element_type=F32)
        inner = jnp.sum(probs * d_probs, axis=0, keepdims=True)
        d_scores = (probs * (d_probs - inner) * scaling).astype(BF16)
        d_keys = jnp.dot(d_scores, queries_spread, preferred_element_type=F32)
        turned = dot(keys, d_scores, TN)
        d_queries = jnp.concatenate([
            turned[head * HEAD_WIDTH:(head + 1) * HEAD_WIDTH, head * TOKENS:(head + 1) * TOKENS]
            for head in range(GROUP)
        ], axis=0).T
        for where, block in ((0, d_queries), (1, d_keys), (2, d_vals)):
            start = where * WIDTH + group * LANES
            factors_ref[:, start:start + LANES] = block.astype(BF16)


def weight_rows(unit, turned_ref, factors_ref):
    turned_ref[...] = unit.T.reshape(turned_ref.shape)
    turned = turned_ref[:, pl.ds(lax.axis_index("c"), 1)].reshape(WIDTH // 2, TOKENS).astype(BF16)
    left = lax.broadcasted_iota(jnp.int32, (128, 128), 1) < 64
    for pair in range(4):
        columns = factors_ref[:, pair * 384:(pair + 1) * 384]
        block = jnp.dot(turned, columns, preferred_element_type=F32)
        middle = block[:, 128:256]
        swapped = pltpu.roll(middle, 64, 1)
        yield 2 * pair, block[:, :128], jnp.where(left, middle[:128], swapped[128:])
        yield 2 * pair + 1, block[:, 256:], jnp.where(left, swapped[:128], middle[128:])


TURNED = (WIDTH // 16, 2, 8, TOKENS)


def window_pass(diag, lat, lon, own, w_qkv, w_proj):
    return pl.pallas_call(
        window_kernel,
        out_shape=[
            jax.ShapeDtypeStruct((TOKENS, 4 * WIDTH), BF16),
            jax.ShapeDtypeStruct((TOKENS, WIDTH), F32),
            jax.ShapeDtypeStruct((TOKENS, 128), F32),
        ],
        compiler_params=pltpu.CompilerParams(vmem_limit_bytes=WINDOW),
    )(diag, lat, lon, own, w_qkv, w_proj)


def inputs_kernel(
    factors_ref, unit_ref, inv_std_ref, w_qkv_ref,
    keep_ref, d_own_ref, d_side_ref, d_lat_ref, turned_ref,
):
    unit = unit_ref[...]
    for index, whole, folded in weight_rows(unit, turned_ref, factors_ref):
        keep_ref[index, :256, :] = whole
        keep_ref[index, 256:, :] = folded
    d_normed = dot(factors_ref[:, :3 * WIDTH], w_qkv_ref[...], NT)
    d_inputs = inv_std_ref[:, :1] * (
        d_normed
        - jnp.mean(d_normed, axis=-1, keepdims=True)
        - unit * jnp.mean(d_normed * unit, axis=-1, keepdims=True)
    )
    d_refs = (d_own_ref, d_side_ref.at[0], d_lat_ref, d_side_ref.at[1])
    for index, ref in enumerate(d_refs):
        block = d_inputs[index * PIECE:(index + 1) * PIECE]
        ref[...] = block.reshape(3, 6, 2, WIDTH).astype(BF16)


def inputs_pass(factors, unit, inv_std, w_qkv):
    weight = jax.ShapeDtypeStruct((8, 384, 128), F32)
    piece = jax.ShapeDtypeStruct((3, 6, 2, WIDTH), BF16)
    side = jax.ShapeDtypeStruct((2, 3, 6, 2, WIDTH), BF16)
    return pl.pallas_call(
        inputs_kernel,
        out_shape=[weight, piece, side, piece],
        scratch_shapes=[pltpu.VMEM(TURNED, F32)],
        compiler_params=SMALL,
    )(factors, unit, inv_std, w_qkv)


def add_kernel(keep_ref, taken_ref, side_in, out_ref, side_out, hold_ref, turned_ref, sems):
    stores = []
    unit = taken_ref[:, 3 * WIDTH:].astype(F32)
    for index, whole, folded in weight_rows(unit, turned_ref, taken_ref):
        hold_ref[index, :256, :] = (keep_ref[index, :256, :] + whole).astype(BF16)
        hold_ref[index, 256:, :] = (keep_ref[index, 256:, :] + folded).astype(BF16)
        store = pltpu.make_async_copy(hold_ref.at[index], out_ref.at[index], sems.at[index])
        store.start()
        stores.append(store)
    for store in stores:
        store.wait()


def add(keep, taken, side):
    vmem = pl.BlockSpec(memory_space=pltpu.VMEM)
    anywhere = pl.BlockSpec(memory_space=pl.ANY)
    return pl.pallas_call(
        add_kernel,
        out_shape=[
            jax.ShapeDtypeStruct(keep.shape, BF16), jax.ShapeDtypeStruct(side.shape, BF16)
        ],
        in_specs=[vmem] * 2 + [anywhere],
        out_specs=[anywhere] * 2,
        input_output_aliases={2: 1},
        scratch_shapes=[
            pltpu.VMEM(keep.shape, BF16),
            pltpu.VMEM(TURNED, F32),
            pltpu.SemaphoreType.DMA((8,)),
        ],
        compiler_params=SMALL,
    )(keep, taken, side)


def finish_kernel(
    grads_ref, own_ref, side_ref, ahead_ref, rows_ref, d_tokens_ref, d_weight_ref
):
    for ref, row, side in (
        (ahead_ref.at[1], 3, 6), (side_ref.at[0], 0, 6), (ahead_ref.at[0], 3, 0), (own_ref, 0, 0)
    ):
        block = grads_ref[row:row + 3, side:side + 6].astype(F32)
        d_tokens_ref[row:row + 3, side:side + 6] = (block + ref[...].astype(F32)).astype(BF16)
    total = jnp.sum(rows_ref[...].astype(F32), axis=0)

    odd = lax.axis_index("x") % 2

    @pl.when(odd == 0)
    def _():
        d_weight_ref[...] = total

    @pl.when(odd == 1)
    def _():
        d_weight_ref[:, :64] = total[:, 128:]
        d_weight_ref[:, 64:] = total[:, :128]


def finish(grads, own, side, ahead, rows):
    return pl.pallas_call(
        finish_kernel,
        out_shape=[
            jax.ShapeDtypeStruct(grads.shape, BF16), jax.ShapeDtypeStruct(rows.shape[1:], F32)
        ],
        compiler_params=SMALL,
    )(grads, own, side, ahead, rows)


def columns_kernel(parts_ref, lat_in, out_ref, lat_out):
    total = parts_ref[0].astype(F32)
    for index in range(1, 8):
        total = total + parts_ref[index].astype(F32)
    rests = (total[256:], pltpu.roll(total[256:], 64, 1))
    for tile in range(32):
        row, fold = 8 * tile, 256 + 8 * (tile % 16)
        place = LON_ORDER.index(tile)
        out_ref[place, :, :128] = total[row:row + 8].astype(BF16)
        out_ref[place, :, 128:] = rests[tile // 16][fold - 256:fold - 248, :64].astype(BF16)


def columns(parts, lat):
    vmem = pl.BlockSpec(memory_space=pltpu.VMEM)
    anywhere = pl.BlockSpec(memory_space=pl.ANY)
    return pl.pallas_call(
        columns_kernel,
        out_shape=[
            jax.ShapeDtypeStruct((32, 8, 192), BF16), jax.ShapeDtypeStruct(lat.shape, BF16)
        ],
        in_specs=[vmem, anywhere],
        out_specs=[vmem, anywhere],
        input_output_aliases={1: 1},
        compiler_params=SMALL,
    )(parts, lat)


def turn(block, axes, distance):
    count = lax.axis_size(axes)
    return lax.ppermute(block, axes, [(i, (i + distance) % count) for i in range(count)])


def turn_both(block, distance):
    lons, lats = lax.axis_size(LON), lax.axis_size(LAT)
    route = [
        (i * lats + j, (i + distance) % lons * lats + (j + distance) % lats)
        for i in range(lons)
        for j in range(lats)
    ]
    return lax.ppermute(block, LON + LAT, route)


def per_device(tokens, cotangent, w_qkv, w_proj):
    tokens = jnp.transpose(tokens, (1, 2, 0, 3))
    cotangent = jnp.transpose(cotangent, (1, 2, 0, 3))
    to_diag, to_lon, to_lat, own = split(tokens, cotangent)
    diag = turn_both(to_diag, 1)
    lon = turn(to_lon, LON, 1)
    lat = turn(to_lat, LAT, 1)
    w_qkv, w_proj = load(w_qkv, w_proj)
    factors, unit, inv_std = window_pass(diag, lat, lon, own, w_qkv, w_proj)
    taken = lax.ppermute(factors, "c", [(0, 1), (1, 0)])
    keep, d_own, d_side, d_lat = inputs_pass(factors, unit, inv_std, w_qkv)
    chip, d_side = add(keep, taken, d_side)
    by_columns = lax.all_to_all(chip, LAT, 0, 0)
    d_side = turn(d_side, LON, -1)
    rows, d_lat = columns(by_columns, d_lat)
    groups = [[2 * tile + core for tile in LON_ORDER] for core in range(2)]
    by_rows = lax.all_to_all(rows, LON, 0, 0, axis_index_groups=groups)
    d_ahead = turn(jnp.stack((d_lat, d_side[1])), LAT, -1)
    d_tokens, d_weight = finish(cotangent, d_own, d_side, d_ahead, by_rows)
    return (jnp.transpose(d_tokens, (2, 0, 1, 3)), d_weight)


def solution(mesh):
    cut = Mesh(mesh.devices.reshape(4, 8, 2, 2, 4), LON + LAT)
    grid = P(None, LAT, LON, None)
    return jax.shard_map(
        per_device, mesh=cut, in_specs=(grid, grid, P(), P()), out_specs=(grid, P(LON, LAT)),
        check_vma=False,
    )
```

```python
import functools

import jax
import jax.numpy as jnp
from jax import lax
from jax.experimental import pallas as pl
from jax.experimental.pallas import tpu as pltpu
from jax.sharding import Mesh, PartitionSpec as P

HEADS = 16
WIDTH = 512
HEAD_WIDTH = WIDTH // HEADS
QUAD = 18
PIECE = 2 * QUAD
TOKENS = 4 * PIECE
GROUP = 8
LANES = GROUP * HEAD_WIDTH
SPREAD = GROUP * TOKENS
FULL = 54880 * 1024
LOAD = 51 * 1024 * 1024
WINDOW = 32 * 1024 * 1024
SMALL = pltpu.CompilerParams(vmem_limit_bytes=8 * 1024 * 1024)

EPS = 1e-05
NEG = -1e30
LON = ("zh", "y", "c")
LAT = ("zl", "x")
LON_ORDER = [31 - i for i in range(32)]
F32 = jnp.float32
BF16 = jnp.bfloat16

NT = (((1,), (1,)), ((), ()))
TN = (((0,), (0,)), ((), ()))


def dot(a, b, dims):
    return lax.dot_general(a, b, dims, preferred_element_type=F32)


QUARTERS = ((3, 6), (0, 6), (3, 0), (0, 0))


def split_kernel(tokens_ref, grads_ref, *refs):
    *quarter_refs, sems = refs
    copies = []
    for ref, (row, side) in zip(quarter_refs, QUARTERS):
        for array, source in enumerate((tokens_ref, grads_ref)):
            quarter = source.at[row:row + 3, side:side + 6]
            copies.append(pltpu.make_async_copy(quarter, ref.at[array], sems.at[len(copies)]))
    for copy in copies:
        copy.start()
    for copy in copies:
        copy.wait()


def split(tokens, grads):
    return pl.pallas_call(
        split_kernel,
        out_shape=[jax.ShapeDtypeStruct((2, 3, 6, 2, WIDTH), BF16)] * 4,
        in_specs=[pl.BlockSpec(memory_space=pl.ANY)] * 2,
        out_specs=[pl.BlockSpec(memory_space=pltpu.VMEM)] * 4,
        scratch_shapes=[pltpu.SemaphoreType.DMA((8,))],
        compiler_params=pltpu.CompilerParams(vmem_limit_bytes=FULL),
    )(tokens, grads)


def load_kernel(*refs):
    loads = [
        pltpu.make_async_copy(refs[index], refs[2 + index], refs[4].at[index])
        for index in range(2)
    ]
    for load in loads:
        load.start()
    for load in loads:
        load.wait()


def load(*arrays):
    return pl.pallas_call(
        load_kernel,
        out_shape=[jax.ShapeDtypeStruct(array.shape, array.dtype) for array in arrays],
        in_specs=[pl.BlockSpec(memory_space=pl.ANY)] * 2,
        out_specs=[pl.BlockSpec(memory_space=pltpu.VMEM)] * 2,
        scratch_shapes=[pltpu.SemaphoreType.DMA((2,))],
        compiler_params=pltpu.CompilerParams(vmem_limit_bytes=LOAD),
    )(*arrays)


def window_kernel(
    diag_ref, lat_ref, lon_ref, own_ref, w_qkv_ref, w_proj_ref,
    factors_ref, unit_ref, inv_std_ref,
):
    pieces = [
        [ref[array].astype(F32).reshape(PIECE, WIDTH) for array in range(2)]
        for ref in (own_ref, lon_ref, lat_ref, diag_ref)
    ]
    values = jnp.concatenate([piece[0] for piece in pieces], axis=0)
    grads = jnp.concatenate([piece[1] for piece in pieces], axis=0).astype(BF16)
    means = jnp.mean(values, axis=-1, keepdims=True)
    centred = values - means
    inv_std = lax.rsqrt(jnp.mean(centred * centred, axis=-1, keepdims=True) + EPS)
    unit = centred * inv_std
    unit_ref[...] = unit
    inv_std_ref[...] = jnp.broadcast_to(inv_std, inv_std_ref.shape)
    normed = unit.astype(BF16)
    factors_ref[:, 3 * WIDTH:] = owned(normed, 1 - lax.axis_index("c")).astype(BF16)
    qkv = jnp.dot(normed, w_qkv_ref[...], preferred_element_type=F32).astype(BF16)
    d_att = dot(grads, w_proj_ref[...], NT).astype(BF16)

    last = (lax.axis_index(LAT) == 0).astype(jnp.int32)

    def region(index):
        quad = index // PIECE
        level = index % 2
        return level + jnp.where(quad >= 2, 2 * last, 0)

    key_region = region(lax.broadcasted_iota(jnp.int32, (TOKENS, 1), 0))
    query_region = region(lax.broadcasted_iota(jnp.int32, (1, SPREAD), 1) % TOKENS)
    allowed = key_region == query_region
    column_head = lax.broadcasted_iota(jnp.int32, (1, LANES), 1) // HEAD_WIDTH
    masks = [(column_head == head).astype(F32).astype(BF16) for head in range(GROUP)]
    scaling = HEAD_WIDTH ** (-0.5)

    for group in range(HEADS // GROUP):
        part = slice(group * LANES, (group + 1) * LANES)
        queries = qkv[:, part]
        keys = qkv[:, WIDTH + group * LANES:WIDTH + (group + 1) * LANES]
        vals = qkv[:, 2 * WIDTH + group * LANES:2 * WIDTH + (group + 1) * LANES]
        outer = d_att[:, part]
        queries_spread = jnp.concatenate([queries * mask for mask in masks], axis=0)
        outer_spread = jnp.concatenate([outer * mask for mask in masks], axis=0)
        scores = dot(keys, queries_spread, NT) * scaling
        scores = jnp.where(allowed, scores, NEG)
        peak = jnp.max(scores, axis=0, keepdims=True)
        expo = jnp.exp(scores - peak)
        probs = expo * (1.0 / jnp.sum(expo, axis=0, keepdims=True))
        d_probs = dot(vals, outer_spread, NT)
        d_vals = jnp.dot(probs.astype(BF16), outer_spread, preferred_element_type=F32)
        inner = jnp.sum(probs * d_probs, axis=0, keepdims=True)
        d_scores = (probs * (d_probs - inner) * scaling).astype(BF16)
        d_keys = jnp.dot(d_scores, queries_spread, preferred_element_type=F32)
        turned = dot(keys, d_scores, TN)
        d_queries = jnp.concatenate([
            turned[head * HEAD_WIDTH:(head + 1) * HEAD_WIDTH, head * TOKENS:(head + 1) * TOKENS]
            for head in range(GROUP)
        ], axis=0).T
        for where, block in ((0, d_queries), (1, d_keys), (2, d_vals)):
            start = where * WIDTH + group * LANES
            factors_ref[:, start:start + LANES] = block.astype(BF16)


def owned(normed, core):
    feature = lax.broadcasted_iota(jnp.int32, (WIDTH, WIDTH // 2), 0)
    place = lax.broadcasted_iota(jnp.int32, (WIDTH, WIDTH // 2), 1)
    chosen = feature == place // 8 * 16 + core * 8 + place % 8
    return jnp.dot(normed, chosen.astype(F32).astype(BF16), preferred_element_type=F32)


def weight_rows(features, factors_ref):
    turned = features.T.astype(BF16)
    left = lax.broadcasted_iota(jnp.int32, (128, 128), 1) < 64
    for pair in range(4):
        columns = factors_ref[:, pair * 384:(pair + 1) * 384]
        block = jnp.dot(turned, columns, preferred_element_type=F32)
        middle = block[:, 128:256]
        swapped = pltpu.roll(middle, 64, 1)
        yield 2 * pair, block[:, :128], jnp.where(left, middle[:128], swapped[128:])
        yield 2 * pair + 1, block[:, 256:], jnp.where(left, swapped[:128], middle[128:])


def window_pass(diag, lat, lon, own, w_qkv, w_proj):
    return pl.pallas_call(
        window_kernel,
        out_shape=[
            jax.ShapeDtypeStruct((TOKENS, 3 * WIDTH + WIDTH // 2), BF16),
            jax.ShapeDtypeStruct((TOKENS, WIDTH), F32),
            jax.ShapeDtypeStruct((TOKENS, 128), F32),
        ],
        compiler_params=pltpu.CompilerParams(vmem_limit_bytes=WINDOW),
    )(diag, lat, lon, own, w_qkv, w_proj)


def inputs_kernel(
    factors_ref, unit_ref, inv_std_ref, w_qkv_ref,
    keep_ref, d_own_ref, d_side_ref, d_lat_ref,
):
    unit = unit_ref[...]
    features = owned(unit.astype(BF16), lax.axis_index("c"))
    for index, whole, folded in weight_rows(features, factors_ref):
        keep_ref[index, :256, :] = whole
        keep_ref[index, 256:, :] = folded
    d_normed = dot(factors_ref[:, :3 * WIDTH], w_qkv_ref[...], NT)
    d_inputs = inv_std_ref[:, :1] * (
        d_normed
        - jnp.mean(d_normed, axis=-1, keepdims=True)
        - unit * jnp.mean(d_normed * unit, axis=-1, keepdims=True)
    )
    d_refs = (d_own_ref, d_side_ref.at[0], d_lat_ref, d_side_ref.at[1])
    for index, ref in enumerate(d_refs):
        block = d_inputs[index * PIECE:(index + 1) * PIECE]
        ref[...] = block.reshape(3, 6, 2, WIDTH).astype(BF16)


def inputs_pass(factors, unit, inv_std, w_qkv):
    weight = jax.ShapeDtypeStruct((8, 384, 128), F32)
    piece = jax.ShapeDtypeStruct((3, 6, 2, WIDTH), BF16)
    side = jax.ShapeDtypeStruct((2, 3, 6, 2, WIDTH), BF16)
    return pl.pallas_call(
        inputs_kernel,
        out_shape=[weight, piece, side, piece],
        compiler_params=SMALL,
    )(factors, unit, inv_std, w_qkv)


def add_kernel(keep_ref, taken_ref, side_in, out_ref, side_out, hold_ref, sems):
    stores = []
    features = taken_ref[:, 3 * WIDTH:].astype(F32)
    for index, whole, folded in weight_rows(features, taken_ref):
        hold_ref[index, :256, :] = (keep_ref[index, :256, :] + whole).astype(BF16)
        hold_ref[index, 256:, :] = (keep_ref[index, 256:, :] + folded).astype(BF16)
        store = pltpu.make_async_copy(hold_ref.at[index], out_ref.at[index], sems.at[index])
        store.start()
        stores.append(store)
    for store in stores:
        store.wait()


def add(keep, taken, side):
    vmem = pl.BlockSpec(memory_space=pltpu.VMEM)
    anywhere = pl.BlockSpec(memory_space=pl.ANY)
    return pl.pallas_call(
        add_kernel,
        out_shape=[
            jax.ShapeDtypeStruct(keep.shape, BF16), jax.ShapeDtypeStruct(side.shape, BF16)
        ],
        in_specs=[vmem] * 2 + [anywhere],
        out_specs=[anywhere] * 2,
        input_output_aliases={2: 1},
        scratch_shapes=[
            pltpu.VMEM(keep.shape, BF16),
            pltpu.SemaphoreType.DMA((8,)),
        ],
        compiler_params=SMALL,
    )(keep, taken, side)


def finish_kernel(
    grads_ref, own_ref, side_ref, ahead_ref, rows_ref, d_tokens_ref, d_weight_ref
):
    for ref, row, side in (
        (ahead_ref.at[1], 3, 6), (side_ref.at[0], 0, 6), (ahead_ref.at[0], 3, 0), (own_ref, 0, 0)
    ):
        block = grads_ref[row:row + 3, side:side + 6].astype(F32)
        d_tokens_ref[row:row + 3, side:side + 6] = (block + ref[...].astype(F32)).astype(BF16)
    total = jnp.sum(rows_ref[...].astype(F32), axis=0)

    odd = lax.axis_index("x") % 2

    @pl.when(odd == 0)
    def _():
        d_weight_ref[...] = total

    @pl.when(odd == 1)
    def _():
        d_weight_ref[:, :64] = total[:, 128:]
        d_weight_ref[:, 64:] = total[:, :128]


def finish(grads, own, side, ahead, rows):
    return pl.pallas_call(
        finish_kernel,
        out_shape=[
            jax.ShapeDtypeStruct(grads.shape, BF16), jax.ShapeDtypeStruct(rows.shape[1:], F32)
        ],
        compiler_params=SMALL,
    )(grads, own, side, ahead, rows)


def columns_kernel(parts_ref, lat_in, out_ref, lat_out):
    total = parts_ref[0].astype(F32)
    for index in range(1, 8):
        total = total + parts_ref[index].astype(F32)
    rests = (total[256:], pltpu.roll(total[256:], 64, 1))
    for tile in range(32):
        row, fold = 8 * tile, 256 + 8 * (tile % 16)
        place = LON_ORDER.index(tile)
        out_ref[place, :, :128] = total[row:row + 8].astype(BF16)
        out_ref[place, :, 128:] = rests[tile // 16][fold - 256:fold - 248, :64].astype(BF16)


def columns(parts, lat):
    vmem = pl.BlockSpec(memory_space=pltpu.VMEM)
    anywhere = pl.BlockSpec(memory_space=pl.ANY)
    return pl.pallas_call(
        columns_kernel,
        out_shape=[
            jax.ShapeDtypeStruct((32, 8, 192), BF16), jax.ShapeDtypeStruct(lat.shape, BF16)
        ],
        in_specs=[vmem, anywhere],
        out_specs=[vmem, anywhere],
        input_output_aliases={1: 1},
        compiler_params=SMALL,
    )(parts, lat)


def turn(block, axes, distance):
    count = lax.axis_size(axes)
    return lax.ppermute(block, axes, [(i, (i + distance) % count) for i in range(count)])


def turn_both(block, distance):
    lons, lats = lax.axis_size(LON), lax.axis_size(LAT)
    route = [
        (i * lats + j, (i + distance) % lons * lats + (j + distance) % lats)
        for i in range(lons)
        for j in range(lats)
    ]
    return lax.ppermute(block, LON + LAT, route)


def per_device(tokens, cotangent, w_qkv, w_proj):
    tokens = jnp.transpose(tokens, (1, 2, 0, 3))
    cotangent = jnp.transpose(cotangent, (1, 2, 0, 3))
    to_diag, to_lon, to_lat, own = split(tokens, cotangent)
    diag = turn_both(to_diag, 1)
    lon = turn(to_lon, LON, 1)
    lat = turn(to_lat, LAT, 1)
    w_qkv, w_proj = load(w_qkv, w_proj)
    factors, unit, inv_std = window_pass(diag, lat, lon, own, w_qkv, w_proj)
    taken = lax.ppermute(factors, "c", [(0, 1), (1, 0)])
    keep, d_own, d_side, d_lat = inputs_pass(factors, unit, inv_std, w_qkv)
    chip, d_side = add(keep, taken, d_side)
    by_columns = lax.all_to_all(chip, LAT, 0, 0)
    d_side = turn(d_side, LON, -1)
    rows, d_lat = columns(by_columns, d_lat)
    groups = [[2 * tile + core for tile in LON_ORDER] for core in range(2)]
    by_rows = lax.all_to_all(rows, LON, 0, 0, axis_index_groups=groups)
    d_ahead = turn(jnp.stack((d_lat, d_side[1])), LAT, -1)
    d_tokens, d_weight = finish(cotangent, d_own, d_side, d_ahead, by_rows)
    return (jnp.transpose(d_tokens, (2, 0, 1, 3)), d_weight)


def solution(mesh):
    cut = Mesh(mesh.devices.reshape(4, 8, 2, 2, 4), LON + LAT)
    grid = P(None, LAT, LON, None)
    return jax.shard_map(
        per_device, mesh=cut, in_specs=(grid, grid, P(), P()), out_specs=(grid, P(LON, LAT)),
        check_vma=False,
    )
```

```python
import functools

import jax
import jax.numpy as jnp
from jax import lax
from jax.experimental import pallas as pl
from jax.experimental.pallas import tpu as pltpu
from jax.sharding import Mesh, PartitionSpec as P

HEADS = 16
WIDTH = 512
HEAD_WIDTH = WIDTH // HEADS
QUAD = 18
PIECE = 2 * QUAD
TOKENS = 4 * PIECE
GROUP = 8
LANES = GROUP * HEAD_WIDTH
SPREAD = GROUP * TOKENS
FULL = 54880 * 1024
LOAD = 51 * 1024 * 1024
WINDOW = 32 * 1024 * 1024
SMALL = pltpu.CompilerParams(vmem_limit_bytes=8 * 1024 * 1024)

EPS = 1e-05
NEG = -1e30
LON = ("zh", "y", "c")
LAT = ("zl", "x")
LON_ORDER = [31 - i for i in range(32)]
F32 = jnp.float32
BF16 = jnp.bfloat16

NT = (((1,), (1,)), ((), ()))
TN = (((0,), (0,)), ((), ()))


def dot(a, b, dims):
    return lax.dot_general(a, b, dims, preferred_element_type=F32)


QUARTERS = ((3, 6), (0, 6), (3, 0), (0, 0))


def split_kernel(tokens_ref, grads_ref, *refs):
    *quarter_refs, sems = refs
    copies = []
    for ref, (row, side) in zip(quarter_refs, QUARTERS):
        for array, source in enumerate((tokens_ref, grads_ref)):
            quarter = source.at[row:row + 3, side:side + 6]
            copies.append(pltpu.make_async_copy(quarter, ref.at[array], sems.at[len(copies)]))
    for copy in copies:
        copy.start()
    for copy in copies:
        copy.wait()


def split(tokens, grads):
    return pl.pallas_call(
        split_kernel,
        out_shape=[jax.ShapeDtypeStruct((2, 3, 6, 2, WIDTH), BF16)] * 4,
        in_specs=[pl.BlockSpec(memory_space=pl.ANY)] * 2,
        out_specs=[pl.BlockSpec(memory_space=pltpu.VMEM)] * 4,
        scratch_shapes=[pltpu.SemaphoreType.DMA((8,))],
        compiler_params=pltpu.CompilerParams(vmem_limit_bytes=FULL),
    )(tokens, grads)


def load_kernel(*refs):
    loads = [
        pltpu.make_async_copy(refs[index], refs[2 + index], refs[4].at[index])
        for index in range(2)
    ]
    for load in loads:
        load.start()
    for load in loads:
        load.wait()


def load(*arrays):
    return pl.pallas_call(
        load_kernel,
        out_shape=[jax.ShapeDtypeStruct(array.shape, array.dtype) for array in arrays],
        in_specs=[pl.BlockSpec(memory_space=pl.ANY)] * 2,
        out_specs=[pl.BlockSpec(memory_space=pltpu.VMEM)] * 2,
        scratch_shapes=[pltpu.SemaphoreType.DMA((2,))],
        compiler_params=pltpu.CompilerParams(vmem_limit_bytes=LOAD),
    )(*arrays)


def window_kernel(
    diag_ref, lat_ref, lon_ref, own_ref, w_qkv_ref, w_proj_ref,
    factors_ref, unit_ref, inv_std_ref,
):
    pieces = [
        [ref[array].astype(F32).reshape(PIECE, WIDTH) for array in range(2)]
        for ref in (own_ref, lon_ref, lat_ref, diag_ref)
    ]
    values = jnp.concatenate([piece[0] for piece in pieces], axis=0)
    grads = jnp.concatenate([piece[1] for piece in pieces], axis=0).astype(BF16)
    means = jnp.mean(values, axis=-1, keepdims=True)
    centred = values - means
    inv_std = lax.rsqrt(jnp.mean(centred * centred, axis=-1, keepdims=True) + EPS)
    unit = centred * inv_std
    unit_ref[...] = unit
    inv_std_ref[...] = jnp.broadcast_to(inv_std, inv_std_ref.shape)
    normed = unit.astype(BF16)
    factors_ref[:, 3 * WIDTH:] = owned(normed, 1 - lax.axis_index("c")).astype(BF16)
    qkv = jnp.dot(normed, w_qkv_ref[...], preferred_element_type=F32).astype(BF16)
    d_att = dot(grads, w_proj_ref[...], NT).astype(BF16)

    last = (lax.axis_index(LAT) == 0).astype(jnp.int32)

    def region(index):
        quad = index // PIECE
        level = index % 2
        return level + jnp.where(quad >= 2, 2 * last, 0)

    key_region = region(lax.broadcasted_iota(jnp.int32, (TOKENS, 1), 0))
    query_region = region(lax.broadcasted_iota(jnp.int32, (1, SPREAD), 1) % TOKENS)
    allowed = key_region == query_region
    column_head = lax.broadcasted_iota(jnp.int32, (1, LANES), 1) // HEAD_WIDTH
    masks = [(column_head == head).astype(F32).astype(BF16) for head in range(GROUP)]
    scaling = HEAD_WIDTH ** (-0.5)

    for group in range(HEADS // GROUP):
        part = slice(group * LANES, (group + 1) * LANES)
        queries = qkv[:, part]
        keys = qkv[:, WIDTH + group * LANES:WIDTH + (group + 1) * LANES]
        vals = qkv[:, 2 * WIDTH + group * LANES:2 * WIDTH + (group + 1) * LANES]
        outer = d_att[:, part]
        queries_spread = jnp.concatenate([queries * mask for mask in masks], axis=0)
        outer_spread = jnp.concatenate([outer * mask for mask in masks], axis=0)
        scores = dot(keys, queries_spread, NT) * scaling
        scores = jnp.where(allowed, scores, NEG)
        peak = jnp.max(scores, axis=0, keepdims=True)
        expo = jnp.exp(scores - peak)
        probs = expo * (1.0 / jnp.sum(expo, axis=0, keepdims=True))
        d_probs = dot(vals, outer_spread, NT)
        d_vals = jnp.dot(probs.astype(BF16), outer_spread, preferred_element_type=F32)
        inner = jnp.sum(probs * d_probs, axis=0, keepdims=True)
        d_scores = (probs * (d_probs - inner) * scaling).astype(BF16)
        d_keys = jnp.dot(d_scores, queries_spread, preferred_element_type=F32)
        turned = dot(keys, d_scores, TN)
        d_queries = jnp.concatenate([
            turned[head * HEAD_WIDTH:(head + 1) * HEAD_WIDTH, head * TOKENS:(head + 1) * TOKENS]
            for head in range(GROUP)
        ], axis=0).T
        for where, block in ((0, d_queries), (1, d_keys), (2, d_vals)):
            start = where * WIDTH + group * LANES
            factors_ref[:, start:start + LANES] = block.astype(BF16)


def owned(normed, core):
    feature = lax.broadcasted_iota(jnp.int32, (WIDTH, WIDTH // 2), 0)
    place = lax.broadcasted_iota(jnp.int32, (WIDTH, WIDTH // 2), 1)
    chosen = feature == place // 8 * 16 + core * 8 + place % 8
    return jnp.dot(normed, chosen.astype(F32).astype(BF16), preferred_element_type=F32)


def weight_rows(features, factors_ref):
    turned = features.T.astype(BF16)
    left = lax.broadcasted_iota(jnp.int32, (128, 128), 1) < 64
    for pair in range(4):
        columns = factors_ref[:, pair * 384:(pair + 1) * 384]
        block = jnp.dot(turned, columns, preferred_element_type=F32)
        middle = block[:, 128:256]
        swapped = pltpu.roll(middle, 64, 1)
        yield 2 * pair, block[:, :128], jnp.where(left, middle[:128], swapped[128:])
        yield 2 * pair + 1, block[:, 256:], jnp.where(left, swapped[:128], middle[128:])


def window_pass(diag, lat, lon, own, w_qkv, w_proj):
    return pl.pallas_call(
        window_kernel,
        out_shape=[
            jax.ShapeDtypeStruct((TOKENS, 3 * WIDTH + WIDTH // 2), BF16),
            jax.ShapeDtypeStruct((TOKENS, WIDTH), F32),
            jax.ShapeDtypeStruct((TOKENS, 128), F32),
        ],
        compiler_params=pltpu.CompilerParams(vmem_limit_bytes=WINDOW),
    )(diag, lat, lon, own, w_qkv, w_proj)


def inputs_kernel(
    factors_ref, unit_ref, inv_std_ref, w_qkv_ref,
    keep_ref, d_own_ref, d_side_ref, d_lat_ref,
):
    unit = unit_ref[...]
    features = owned(unit.astype(BF16), lax.axis_index("c"))
    for index, whole, folded in weight_rows(features, factors_ref):
        keep_ref[index, :256, :] = whole
        keep_ref[index, 256:, :] = folded
    d_normed = dot(factors_ref[:, :3 * WIDTH], w_qkv_ref[...], NT)
    d_inputs = inv_std_ref[:, :1] * (
        d_normed
        - jnp.mean(d_normed, axis=-1, keepdims=True)
        - unit * jnp.mean(d_normed * unit, axis=-1, keepdims=True)
    )
    d_refs = (d_own_ref, d_side_ref.at[0], d_lat_ref, d_side_ref.at[1])
    for index, ref in enumerate(d_refs):
        block = d_inputs[index * PIECE:(index + 1) * PIECE]
        ref[...] = block.reshape(3, 6, 2, WIDTH).astype(BF16)


def inputs_pass(factors, unit, inv_std, w_qkv):
    weight = jax.ShapeDtypeStruct((8, 384, 128), F32)
    piece = jax.ShapeDtypeStruct((3, 6, 2, WIDTH), BF16)
    side = jax.ShapeDtypeStruct((2, 3, 6, 2, WIDTH), BF16)
    return pl.pallas_call(
        inputs_kernel,
        out_shape=[weight, piece, side, piece],
        compiler_params=SMALL,
    )(factors, unit, inv_std, w_qkv)


def add_kernel(keep_ref, taken_ref, side_in, out_ref, side_out, hold_ref, sems):
    stores = []
    features = taken_ref[:, 3 * WIDTH:].astype(F32)
    for index, whole, folded in weight_rows(features, taken_ref):
        hold_ref[index, :256, :] = (keep_ref[index, :256, :] + whole).astype(BF16)
        hold_ref[index, 256:, :] = (keep_ref[index, 256:, :] + folded).astype(BF16)
        store = pltpu.make_async_copy(hold_ref.at[index], out_ref.at[index], sems.at[index])
        store.start()
        stores.append(store)
    for store in stores:
        store.wait()


def add(keep, taken, side):
    vmem = pl.BlockSpec(memory_space=pltpu.VMEM)
    anywhere = pl.BlockSpec(memory_space=pl.ANY)
    return pl.pallas_call(
        add_kernel,
        out_shape=[
            jax.ShapeDtypeStruct(keep.shape, BF16), jax.ShapeDtypeStruct(side.shape, BF16)
        ],
        in_specs=[vmem] * 2 + [anywhere],
        out_specs=[anywhere] * 2,
        input_output_aliases={2: 1},
        scratch_shapes=[
            pltpu.VMEM(keep.shape, BF16),
            pltpu.SemaphoreType.DMA((8,)),
        ],
        compiler_params=SMALL,
    )(keep, taken, side)


def finish_kernel(
    grads_ref, own_ref, side_ref, ahead_ref, rows_ref, d_tokens_ref, d_weight_ref
):
    for ref, row, side in (
        (ahead_ref.at[1], 3, 6), (side_ref.at[0], 0, 6), (ahead_ref.at[0], 3, 0), (own_ref, 0, 0)
    ):
        block = grads_ref[row:row + 3, side:side + 6].astype(F32)
        d_tokens_ref[row:row + 3, side:side + 6] = (block + ref[...].astype(F32)).astype(BF16)
    total = jnp.sum(rows_ref[...].astype(F32), axis=0)

    odd = lax.axis_index("x") % 2

    @pl.when(odd == 0)
    def _():
        d_weight_ref[...] = total

    @pl.when(odd == 1)
    def _():
        d_weight_ref[:, :64] = total[:, 128:]
        d_weight_ref[:, 64:] = total[:, :128]


def finish(grads, own, side, ahead, rows):
    return pl.pallas_call(
        finish_kernel,
        out_shape=[
            jax.ShapeDtypeStruct(grads.shape, BF16), jax.ShapeDtypeStruct(rows.shape[1:], F32)
        ],
        compiler_params=SMALL,
    )(grads, own, side, ahead, rows)


def columns_kernel(parts_ref, out_ref):
    total = parts_ref[0].astype(F32)
    for index in range(1, 8):
        total = total + parts_ref[index].astype(F32)
    rests = (total[256:], pltpu.roll(total[256:], 64, 1))
    for tile in range(32):
        row, fold = 8 * tile, 256 + 8 * (tile % 16)
        place = LON_ORDER.index(tile)
        out_ref[place, :, :128] = total[row:row + 8].astype(BF16)
        out_ref[place, :, 128:] = rests[tile // 16][fold - 256:fold - 248, :64].astype(BF16)


def columns(parts):
    return pl.pallas_call(
        columns_kernel,
        out_shape=jax.ShapeDtypeStruct((32, 8, 192), BF16),
        compiler_params=SMALL,
    )(parts)


def turn(block, axes, distance):
    count = lax.axis_size(axes)
    return lax.ppermute(block, axes, [(i, (i + distance) % count) for i in range(count)])


def turn_both(block, distance):
    lons, lats = lax.axis_size(LON), lax.axis_size(LAT)
    route = [
        (i * lats + j, (i + distance) % lons * lats + (j + distance) % lats)
        for i in range(lons)
        for j in range(lats)
    ]
    return lax.ppermute(block, LON + LAT, route)


def per_device(tokens, cotangent, w_qkv, w_proj):
    tokens = jnp.transpose(tokens, (1, 2, 0, 3))
    cotangent = jnp.transpose(cotangent, (1, 2, 0, 3))
    to_diag, to_lon, to_lat, own = split(tokens, cotangent)
    diag = turn_both(to_diag, 1)
    lon = turn(to_lon, LON, 1)
    lat = turn(to_lat, LAT, 1)
    w_qkv, w_proj = load(w_qkv, w_proj)
    factors, unit, inv_std = window_pass(diag, lat, lon, own, w_qkv, w_proj)
    taken = lax.ppermute(factors, "c", [(0, 1), (1, 0)])
    keep, d_own, d_side, d_lat = inputs_pass(factors, unit, inv_std, w_qkv)
    chip, d_side = add(keep, taken, d_side)
    by_columns = lax.all_to_all(chip, LAT, 0, 0)
    d_side = turn(d_side, LON, -1)
    rows = columns(by_columns)
    groups = [[2 * tile + core for tile in LON_ORDER] for core in range(2)]
    by_rows = lax.all_to_all(rows, LON, 0, 0, axis_index_groups=groups)
    d_ahead = turn(jnp.stack((d_lat, d_side[1])), LAT, -1)
    d_tokens, d_weight = finish(cotangent, d_own, d_side, d_ahead, by_rows)
    return (jnp.transpose(d_tokens, (2, 0, 1, 3)), d_weight)


def solution(mesh):
    cut = Mesh(mesh.devices.reshape(4, 8, 2, 2, 4), LON + LAT)
    grid = P(None, LAT, LON, None)
    return jax.shard_map(
        per_device, mesh=cut, in_specs=(grid, grid, P(), P()), out_specs=(grid, P(LON, LAT)),
        check_vma=False,
    )
```
